32 devices in a mesh: slab: 8 (over z, y), sub: 4 (over x, core).
Axes of the slice: x: 2, y: 2, z: 4, core: 2. Of those that a mesh axis runs over, the one named last changes fastest.
Arguments:
- mode_shapes: bfloat16 [32, 6, 64, 512], P(None, None, 'slab', 'sub')
- span_stiff: float32 [6, 64, 512], P(None, 'slab', 'sub'), may hold values from -4 to 4
- chord_stiff: float32 [6, 64, 512], P(None, 'slab', 'sub'), may hold values from -4 to 4
- span_geo: float32 [64, 512], P('slab', 'sub'), may hold values from 0.2 to 2
- chord_geo: float32 [64, 512], P('slab', 'sub'), may hold values from 0.2 to 2
- ground: float32 [6, 64, 512], P(None, 'slab', 'sub'), may hold values from 0.2 to 2
- chord_len: int32 [64], replicated, may hold values from 192 to 512, as said below
Outputs:
- adjoint: float32 [32, 6, 64, 512], P(None, None, 'slab', 'sub')
- residual: float32 [32, 6, 64, 512], P(None, None, 'slab', 'sub')
The draws below stay inside these ranges and needn't reach their ends.
Inputs may be any that keep to these rules, and one draw needn't show every extreme that they name: chord_len[0] = 512.
All inputs are finite; a program needn't handle non-finite values.
Results may differ from the reference program's by a relative error of at most 0.0003.
Values sent between devices are 32-bit elements; how exact they have to be, the bound alone decides.
No kernel may reach another device: no remote copies, remote signals or barrier semaphores. Data moves between devices by JAX's collectives and lax.ppermute only.
A program may use at most 64 MiB of HBM per device.

```python
import math
import jax
import jax.numpy as jnp
from jax import lax

MODES = 32
DOF = 6
ITERS = 2
NS = 64
NC = 512


def draw_mode_shapes(key, part):
    first_key = jax.random.fold_in(key, 0)
    shape_full = (MODES, DOF, NS, NC)
    station = jnp.arange(NS, dtype=jnp.float32) / NS
    amplitude = (0.3 * (0.5 + 1.5 * station))[None, None, :, None]
    values = jnp.clip(jax.random.normal(first_key, shape_full, jnp.float32), -4.0, 4.0)
    return (values * amplitude).astype(jnp.bfloat16)


def draw_chord_len(key, part):
    stations = jnp.arange(NS, dtype=jnp.int32)
    taper = NC // 2 * stations // NS
    jitter = jax.random.randint(key, (NS,), 0, max(NC // 8, 1), dtype=jnp.int32)
    jitter = jnp.where(stations == 0, 0, jitter)
    return (NC - taper - jitter).astype(jnp.int32)


def levels(stream_key, shape, shards, low, top_value):
    factor_of, own = 1.0, jax.random.fold_in(stream_key, 6)
    for dim, blocks in shards:
        heights = jnp.exp(jax.random.uniform(jax.random.fold_in(own, dim), (blocks,), jnp.float32, low / len(shards), top_value / len(shards)))
        factor_of = factor_of * jnp.repeat(heights, shape[dim] // blocks).reshape([-1 if axis == dim else 1 for axis in range(len(shape))])
    return factor_of


def bell_draw(key, extent, spread, bound, cuts=(), kind=jnp.bfloat16):
    values = jax.random.normal(key, extent, jnp.float32) * spread
    if len(cuts) > 0:
        values = levels(key, extent, cuts, -0.22, 0.18) * values
    return jnp.clip(values, min=-bound, max=bound).astype(kind)


def setup_inputs(seed: int = 0) -> dict:
    streams_of = jax.random.split(jax.random.key(seed), 8)
    mode_shapes = draw_mode_shapes(jax.random.fold_in(streams_of[7], 71), 0)
    span_stiff = bell_draw(streams_of[1], (DOF, NS, NC), 0.7, 4.0, ((1, 8), (2, 4)), jnp.float32)
    chord_stiff = bell_draw(streams_of[2], (DOF, NS, NC), 0.7, 4.0, ((1, 8), (2, 4)), jnp.float32)
    span_geo = jnp.clip(jnp.exp(math.log(2.0) - 2.3025851 * jax.random.uniform(streams_of[3], (NS, NC), jnp.float32) ** levels(streams_of[3], (NS, NC), ((0, 8), (1, 4)), -0.2, 0.2)), 0.2, 2.0)
    chord_geo = jnp.clip(jnp.exp(math.log(2.0) - 2.3025851 * jax.random.uniform(streams_of[4], (NS, NC), jnp.float32) ** levels(streams_of[4], (NS, NC), ((0, 8), (1, 4)), -0.2, 0.2)), 0.2, 2.0)
    ground = jnp.clip(jnp.exp(math.log(2.0) - 2.3025851 * jax.random.uniform(streams_of[5], (DOF, NS, NC), jnp.float32) ** levels(streams_of[5], (DOF, NS, NC), ((1, 8), (2, 4)), -0.2, 0.2)), 0.2, 2.0)
    chord_len = draw_chord_len(jax.random.fold_in(streams_of[7], 71), 0)
    return dict(mode_shapes=mode_shapes, span_stiff=span_stiff, chord_stiff=chord_stiff, span_geo=span_geo, chord_geo=chord_geo, ground=ground, chord_len=chord_len)


def ahead_of(field, along):
    remainder = lax.slice_in_dim(field, 1, field.shape[along], axis=along)
    zero_rim = jnp.zeros_like(lax.slice_in_dim(field, 0, 1, axis=along))
    return jnp.concatenate([remainder, zero_rim], axis=along)

def behind_of(field, along):
    remainder = lax.slice_in_dim(field, 0, field.shape[along] - 1, axis=along)
    zero_rim = jnp.zeros_like(lax.slice_in_dim(field, 0, 1, axis=along))
    return jnp.concatenate([zero_rim, remainder], axis=along)

def edge_masks(chord_len):
    columns = jnp.arange(NC, dtype=jnp.int32)[None, :]
    length_here = chord_len[:, None]
    length_next = jnp.concatenate([chord_len[1:], jnp.zeros((1,), jnp.int32)])[:, None]
    span_live = ((columns < length_here) & (columns < length_next)).astype(jnp.float32)
    chord_live = (columns + 1 < length_here).astype(jnp.float32)
    return (span_live, chord_live)

def node_blocks(span_stiff, chord_stiff, span_live, chord_live, ground):
    count = ground.shape[0]
    blocks = []
    for i in range(count):
        block_row = []
        for j in range(count):
            span_pair = span_stiff[i] * span_stiff[j] * span_live
            chord_pair = chord_stiff[i] * chord_stiff[j] * chord_live
            entry = span_pair + behind_of(span_pair, 0) + chord_pair + behind_of(chord_pair, 1)
            if i == j:
                entry = entry + ground[i]
            block_row.append(entry)
        blocks.append(block_row)
    return blocks

def factor_blocks(blocks):
    count = len(blocks)
    factor = [[None] * count for i in range(count)]
    inverse = [None] * count
    for j in range(count):
        running = blocks[j][j]
        for k in range(j):
            running = running - factor[j][k] * factor[j][k]
        diag_root = jnp.sqrt(running)
        factor[j][j] = diag_root
        inverse[j] = 1.0 / diag_root
        for i in range(j + 1, count):
            running = blocks[i][j]
            for k in range(j):
                running = running - factor[i][k] * factor[j][k]
            factor[i][j] = running * inverse[j]
    return (factor, inverse)

def solve_blocks(factor, inverse, vector):
    count = len(inverse)
    forward = []
    for i in range(count):
        running = vector[:, i]
        for j in range(i):
            running = running - factor[i][j][None] * forward[j]
        forward.append(running * inverse[i][None])
    backward = [None] * count
    for i in reversed(range(count)):
        running = forward[i]
        for j in range(i + 1, count):
            running = running - factor[j][i][None] * backward[j]
        backward[i] = running * inverse[i][None]
    return jnp.stack(backward, axis=1)

def operate(field, span_stiff, chord_stiff, span_live, chord_live, ground):
    result = ground[None] * field
    for stiffness, live_mask, along in ((span_stiff, span_live, 2), (chord_stiff, chord_live, 3)):
        strain = lax.optimization_barrier(jnp.sum(stiffness[None] * (ahead_of(field, along) - field), axis=1)) * live_mask[None]
        forces = stiffness[None] * strain[:, None]
        result = result - forces + behind_of(forces, along)
    return result

def loads(mode_field, span_stiff, chord_stiff, span_geo, chord_geo, span_live, chord_live):
    result = jnp.zeros_like(mode_field)
    for stiffness, geometric, live_mask, along in ((span_stiff, span_geo, span_live, 2), (chord_stiff, chord_geo, chord_live, 3)):
        jump = ahead_of(mode_field, along) - mode_field
        weight = lax.optimization_barrier(jnp.sum(jump * jump, axis=1)) * (geometric * live_mask)[None]
        forces = stiffness[None] * weight[:, None]
        result = result - forces + behind_of(forces, along)
    return result

def reference(mode_shapes, span_stiff, chord_stiff, span_geo, chord_geo, ground, chord_len):
    mode_field = mode_shapes.astype(jnp.float32)
    span_live, chord_live = edge_masks(chord_len)
    factor, inverse = factor_blocks(node_blocks(span_stiff, chord_stiff, span_live, chord_live, ground))
    load = loads(mode_field, span_stiff, chord_stiff, span_geo, chord_geo, span_live, chord_live)
    solution = jnp.zeros_like(load)
    residual = load
    precond = solve_blocks(factor, inverse, residual)
    direction = precond
    precond_norm = lax.optimization_barrier(jnp.sum(residual * precond, axis=(1, 2, 3)))
    for step in range(ITERS):
        image = operate(direction, span_stiff, chord_stiff, span_live, chord_live, ground)
        step_size = precond_norm / lax.optimization_barrier(jnp.sum(direction * image, axis=(1, 2, 3)))
        solution = solution + step_size[:, None, None, None] * direction
        residual = residual - step_size[:, None, None, None] * image
        if step + 1 < ITERS:
            precond = solve_blocks(factor, inverse, residual)
            norm_next = lax.optimization_barrier(jnp.sum(residual * precond, axis=(1, 2, 3)))
            direction = precond + (norm_next / precond_norm)[:, None, None, None] * direction
            precond_norm = norm_next
    return (solution, residual)
```

```python
import jax
import jax.numpy as jnp
from jax import lax
from jax.experimental import pallas as pl
from jax.experimental.pallas import tpu as pltpu
from jax.sharding import PartitionSpec as P

F32 = jnp.float32
VMEM_LIMIT = 24 * 1024 * 1024


def matching(slabs, subs, along_slab, parity):
    pairs = []
    for s in range(slabs):
        for c in range(subs):
            here, count = (s, slabs) if along_slab else (c, subs)
            there = here + 1 if here % 2 == parity else here - 1
            if 0 <= there < count:
                target = (there, c) if along_slab else (s, there)
            elif along_slab:
                target = (s, c ^ 1) if subs % 2 == 0 else None
            else:
                target = (s, subs - 1 - c) if subs % 2 == 0 else None
            if target is not None:
                pairs.append((s * subs + c, target[0] * subs + target[1]))
    return pairs


def roll(value, shift, axis):
    size = value.shape[axis]
    if isinstance(shift, int):
        return pltpu.roll(value, shift % size, axis)
    return pltpu.roll(value, lax.rem(shift + size, size), axis)


def dot(left, right):
    total = left[0] * right[0]
    for k in range(1, len(left)):
        total = total + left[k] * right[k]
    return total


def axpy4(coefs, values):
    total = coefs[0] * values[0]
    for k in range(1, len(coefs)):
        total = total + coefs[k] * values[k]
    return total


def tile_iota(shape):
    return lax.broadcasted_iota(jnp.int32, shape, 0), lax.broadcasted_iota(jnp.int32, shape, 1)


def parities():
    return lax.rem(lax.axis_index("slab"), 2) == 0, lax.rem(lax.axis_index("sub"), 2) == 0


def pack_kernel(dims, modes_ref, span_ref, chord_ref, span_geo_ref, chord_geo_ref,
                row_even, row_odd, col_even, col_odd, field):
    modes, dof, rows, cols = dims
    row, lane = tile_iota((rows, cols))
    slab_even, sub_even = parities()
    per = dof * rows

    def body(m, carry):
        start = pl.multiple_of(m * per, per)
        block = modes_ref[pl.ds(start, per), :].astype(F32)
        field[pl.ds(start, per), :] = block
        mine = (lane >> 1) == m
        return tuple(
            jnp.where(mine, roll(block[k * rows:(k + 1) * rows], 2 * m + 1, 1), carry[k]) for k in range(dof)
        )

    packed = lax.fori_loop(0, modes, body, tuple(jnp.zeros((rows, cols), F32) for k in range(dof)))
    coef = jnp.zeros((rows, cols), F32)
    edge = jnp.zeros((rows, cols), F32)
    for k in range(dof + 1):
        span_plane = span_ref[k] if k < dof else span_geo_ref[...]
        chord_plane = chord_ref[k] if k < dof else chord_geo_ref[...]
        coef = jnp.where(row == k, span_plane[rows - 1:rows], coef)
        edge = jnp.where(lane == 2 * k, roll(chord_plane, 2 * k + 1, 1), edge)
    for k in range(dof):
        behind = roll(packed[k], -1, 1)
        col_even[k * rows:(k + 1) * rows, :] = jnp.where(sub_even, packed[k], behind)
        col_odd[k * rows:(k + 1) * rows, :] = jnp.where(sub_even, behind, packed[k])
        for block in range(modes // 8):
            base = block * 8 * per + k * rows
            first = field[pl.ds(base, 8, stride=per), :]
            last = field[pl.ds(base + rows - 1, 8, stride=per), :]
            out = k * modes + block * 8
            row_even[out:out + 8, :] = jnp.where(slab_even, last, first)
            row_odd[out:out + 8, :] = jnp.where(slab_even, first, last)
    row_even[dof * modes:dof * modes + rows, :] = coef
    row_odd[dof * modes:dof * modes + rows, :] = coef
    col_even[dof * rows:(dof + 1) * rows, :] = edge
    col_odd[dof * rows:(dof + 1) * rows, :] = edge


def factor_blocks(blocks):
    count = len(blocks)
    factor = [[None] * count for i in range(count)]
    inverse = [None] * count
    for j in range(count):
        running = blocks[j][j]
        for k in range(j):
            running = running - factor[j][k] * factor[j][k]
        diag_root = jnp.sqrt(running)
        factor[j][j] = diag_root
        inverse[j] = 1.0 / diag_root
        for i in range(j + 1, count):
            running = blocks[i][j]
            for k in range(j):
                running = running - factor[i][k] * factor[j][k]
            factor[i][j] = running * inverse[j]
    return (factor, inverse)


def invert_blocks(blocks):
    count = len(blocks)
    factor, inverse = factor_blocks(blocks)
    lower = [[None] * count for i in range(count)]
    for j in range(count):
        lower[j][j] = inverse[j]
        for i in range(j + 1, count):
            running = factor[i][j] * lower[j][j]
            for k in range(j + 1, i):
                running = running + factor[i][k] * lower[k][j]
            lower[i][j] = -(running * inverse[i])
    result = [[None] * count for i in range(count)]
    for i in range(count):
        for j in range(i + 1):
            running = lower[i][i] * lower[i][j]
            for k in range(i + 1, count):
                running = running + lower[k][i] * lower[k][j]
            result[i][j] = running
    return result


def apply_inverse(entry, vector):
    count = len(vector)
    return [dot([entry(max(i, j), min(i, j)) for j in range(count)], vector) for i in range(count)]


def first_kernel(dims, sizes, modes_ref, span_ref, chord_ref, span_geo_ref, chord_geo_ref, ground_ref, len_ref,
                 row_even_out, row_odd_out, col_even_out, col_odd_out,
                 row_even_in, row_odd_in, col_even_in, col_odd_in,
                 load_ref, z_ref, q_ref, g_ref, coef_ref, row_even, row_odd, col_even, col_odd,
                 inv_ref, up_ref, down_ref, rim_ref, rim2_ref):
    modes, dof, rows, cols = dims
    slabs, subs = sizes
    row, lane = tile_iota((rows, cols))
    slab_even, sub_even = parities()
    per = dof * rows
    stations = slabs * rows
    row_start = lax.axis_index("slab") * rows
    col_start = lax.axis_index("sub") * cols
    column = col_start + lane

    def length(index):
        value = len_ref[jnp.clip(index, 0, stations - 1)]
        return jnp.where((index >= 0) & (index < stations), value, 0)

    own = jnp.zeros((rows, cols), jnp.int32)
    ahead = jnp.zeros((rows, cols), jnp.int32)
    for r in range(rows):
        own = jnp.where(row == r, length(row_start + r), own)
        ahead = jnp.where(row == r, length(row_start + r + 1), ahead)
    span_live = (column < own) & (column < ahead)
    chord_live = column + 1 < own
    up_live = (column < length(row_start - 1)) & (column < length(row_start))
    left_live = (col_start < own) & (col_start > 0)

    def row_weight(arrived, sent):
        total = None
        for k in range(dof):
            jump = arrived[k * modes:(k + 1) * modes, :] - sent[k * modes:(k + 1) * modes, :]
            total = jump * jump if total is None else total + jump * jump
        return total

    def col_weight(arrived, sent):
        total = None
        for k in range(dof):
            jump = arrived[k * rows:(k + 1) * rows, :] - sent[k * rows:(k + 1) * rows, :]
            total = jump * jump if total is None else total + jump * jump
        return total

    even_weight = row_weight(row_even_in, row_even_out)
    odd_weight = row_weight(row_odd_in, row_odd_out)
    up_weight = jnp.where(slab_even, odd_weight, even_weight)
    down_weight = jnp.where(slab_even, even_weight, odd_weight)
    tail = dof * modes
    up_coef = jnp.where(slab_even, row_odd_in[tail:tail + rows, :], row_even_in[tail:tail + rows, :])
    up_ref[...] = jnp.where(up_live[0:1], up_weight * up_coef[dof:dof + 1], 0.0)
    down_ref[...] = jnp.where(span_live[rows - 1:rows], down_weight * span_geo_ref[rows - 1:rows, :], 0.0)
    even_col = col_weight(col_even_in, col_even_out)
    odd_col = col_weight(col_odd_in, col_odd_out)
    left_coef = jnp.where(sub_even, col_odd_in[per:per + rows, :], col_even_in[per:per + rows, :])
    left_weight = jnp.where(sub_even, odd_col, even_col) * left_coef[:, 2 * dof:2 * dof + 1]
    right_weight = jnp.where(sub_even, even_col, odd_col) * chord_geo_ref[:, cols - 1:cols]
    left_weight = jnp.where(left_live, left_weight, 0.0)
    right_weight = jnp.where(chord_live[:, cols - 1:cols], right_weight, 0.0)
    lane_even = (lane & 1) == 0
    rim_weight = jnp.where(lane_even, left_weight, roll(right_weight, -1, 1))

    first_row, last_row = row == 0, row == rows - 1
    first_col, last_col = lane == 0, lane == cols - 1

    zero = jnp.zeros((rows, cols), F32)
    span, span_b, chord, chord_b = [], [], [], []
    for k in range(dof):
        span.append(jnp.where(span_live, span_ref[k], zero))
        up = jnp.where(up_live, up_coef[k:k + 1], zero)
        span_b.append(jnp.where(first_row, up, roll(span[k], 1, 0)))
        chord.append(jnp.where(chord_live, chord_ref[k], zero))
        left = jnp.where(left_live, left_coef[:, 2 * k:2 * k + 1], zero)
        chord_b.append(jnp.where(first_col, left, roll(chord[k], 1, 1)))
    blocks = [[None] * dof for i in range(dof)]
    for i in range(dof):
        for j in range(i + 1):
            entry = span[i] * span[j] + span_b[i] * span_b[j] + chord[i] * chord[j] + chord_b[i] * chord_b[j]
            blocks[i][j] = entry + ground_ref[i] if i == j else entry
    inv = invert_blocks(blocks)
    place = {}
    for i in range(dof):
        for j in range(i + 1):
            place[i, j] = len(place)
            inv_ref[place[i, j]] = inv[i][j]
    row_rim = [jnp.where(last_row, span[k], jnp.where(first_row, span_b[k], zero)) for k in range(dof)]
    col_rim = [jnp.where(last_col, chord[k], jnp.where(first_col, chord_b[k], zero)) for k in range(dof)]
    row_inv = apply_inverse(lambda i, j: inv[i][j], row_rim)
    col_inv = apply_inverse(lambda i, j: inv[i][j], col_rim)
    for group, planes in enumerate((span, span_b, chord, chord_b, row_rim, col_rim, row_inv, col_inv)):
        for k in range(dof):
            coef_ref[group * dof + k] = planes[k]
    row_kappa = dot(row_rim, row_inv)
    col_kappa = dot(col_rim, col_inv)
    coef_ref[8 * dof] = dot(row_rim, col_inv)

    def planes_of(group):
        return [coef_ref[group * dof + k] for k in range(dof)]

    def body(m, carry):
        start = pl.multiple_of(m * per, per)
        block = modes_ref[pl.ds(start, per), :].astype(F32)
        v = [block[k * rows:(k + 1) * rows] for k in range(dof)]
        down = down_ref[pl.ds(m, 1), :]
        up = up_ref[pl.ds(m, 1), :]
        rim = roll(rim_weight, -2 * m, 1)
        jumps = [roll(v[k], -1, 0) - v[k] for k in range(dof)]
        span_w = jnp.where(last_row, down, dot(jumps, jumps) * span_geo_ref[...])
        jumps = [roll(v[k], -1, 1) - v[k] for k in range(dof)]
        chord_w = jnp.where(last_col, rim, dot(jumps, jumps) * chord_geo_ref[...])
        span_wb = jnp.where(first_row, up, roll(span_w, 1, 0))
        chord_wb = jnp.where(first_col, rim, roll(chord_w, 1, 1))
        span, span_b, chord, chord_b = (planes_of(i) for i in range(4))
        load = [
            (span_b[k] * span_wb - span[k] * span_w) + (chord_b[k] * chord_wb - chord[k] * chord_w)
            for k in range(dof)
        ]
        entry = lambda i, j: inv_ref[place[i, j]]
        z = apply_inverse(entry, load)
        fwd_s, bwd_s, fwd_c, bwd_c = dot(span, z), dot(span_b, z), dot(chord, z), dot(chord_b, z)
        near = [
            jnp.where(last_row, zero, roll(bwd_s, -1, 0)),
            jnp.where(first_row, zero, roll(fwd_s, 1, 0)),
            jnp.where(last_col, zero, roll(bwd_c, -1, 1)),
            jnp.where(first_col, zero, roll(fwd_c, 1, 1)),
        ]
        q = [axpy4([span[k], span_b[k], chord[k], chord_b[k]], near) for k in range(dof)]
        g = apply_inverse(entry, q)
        for k in range(dof):
            at = pl.ds(pl.multiple_of(start + k * rows, rows), rows)
            load_ref[at, :] = load[k]
            z_ref[at, :] = z[k]
            q_ref[at, :] = q[k]
            g_ref[at, :] = g[k]
        at = pl.ds(pl.multiple_of(m * rows, rows), rows)
        rim_ref[at, :] = jnp.where(last_row, fwd_s, bwd_s)
        rim2_ref[at, :] = dot(planes_of(4), g)
        mine = (lane >> 1) == m
        col_z = roll(jnp.where(last_col, fwd_c, bwd_c), 2 * m + 1, 1)
        col_g = roll(dot(planes_of(5), g), 2 * m + 1, 1)
        return jnp.where(mine, col_z, carry[0]), jnp.where(mine, col_g, carry[1])

    col_z, col_g = lax.fori_loop(0, modes, body, (zero, zero))
    for which, packed in enumerate((col_z, col_g, roll(col_kappa, 1, 1))):
        behind = roll(packed, -1, 1)
        col_even[which * rows:(which + 1) * rows, :] = jnp.where(sub_even, packed, behind)
        col_odd[which * rows:(which + 1) * rows, :] = jnp.where(sub_even, behind, packed)
    for which, ref in enumerate((rim_ref, rim2_ref)):
        for block in range(modes // 8):
            first = ref[pl.ds(block * 8 * rows, 8, stride=rows), :]
            last = ref[pl.ds(block * 8 * rows + rows - 1, 8, stride=rows), :]
            out = which * modes + block * 8
            row_even[out:out + 8, :] = jnp.where(slab_even, last, first)
            row_odd[out:out + 8, :] = jnp.where(slab_even, first, last)
    first = jnp.where(first_row, row_kappa[0:1], zero)
    last = jnp.where(first_row, row_kappa[rows - 1:rows], zero)
    row_even[2 * modes:2 * modes + rows, :] = jnp.where(slab_even, last, first)
    row_odd[2 * modes:2 * modes + rows, :] = jnp.where(slab_even, first, last)


def second_kernel(dims, devices, load_ref, z_ref, qp_ref, gp_ref, coef_ref,
                  row_even_out, row_odd_out, col_even_out, col_odd_out,
                  row_even_in, row_odd_in, col_even_in, col_odd_in,
                  q_ref, g_ref, q2_ref, chunk_ref,
                  up_ref, down_ref, up2_ref, down2_ref, sum_ref):
    modes, dof, rows, cols = dims
    row, lane = tile_iota((rows, cols))
    slab_even, sub_even = parities()
    per = dof * rows
    first_row, last_row = row == 0, row == rows - 1
    first_col, last_col = lane == 0, lane == cols - 1
    lane_even = (lane & 1) == 0
    zero = jnp.zeros((rows, cols), F32)

    def pick(flag, even, odd, start, size):
        return jnp.where(flag, even[start:start + size, :], odd[start:start + size, :])

    up_flag = jnp.logical_not(slab_even)
    left_flag = jnp.logical_not(sub_even)
    up_ref[...] = pick(up_flag, row_even_in, row_odd_in, 0, modes)
    down_ref[...] = pick(slab_even, row_even_in, row_odd_in, 0, modes)
    up2_ref[...] = (
        pick(up_flag, row_even_in, row_odd_in, modes, modes)
        + pick(up_flag, row_even_in, row_odd_in, 2 * modes, 1) * pick(up_flag, row_even_out, row_odd_out, 0, modes)
    )
    down2_ref[...] = (
        pick(slab_even, row_even_in, row_odd_in, modes, modes)
        + pick(slab_even, row_even_in, row_odd_in, 2 * modes, 1) * pick(slab_even, row_even_out, row_odd_out, 0, modes)
    )

    def merge(left, right):
        return jnp.where(lane_even, left, roll(right, -1, 1))

    def second_col(flag):
        kappa = pick(flag, col_even_in, col_odd_in, 2 * rows, rows)[:, 0:1]
        return pick(flag, col_even_in, col_odd_in, rows, rows) + kappa * pick(flag, col_even_out, col_odd_out, 0, rows)

    rim = merge(pick(left_flag, col_even_in, col_odd_in, 0, rows), pick(sub_even, col_even_in, col_odd_in, 0, rows))
    rim2 = merge(second_col(left_flag), second_col(sub_even))
    corner_kappa = coef_ref[8 * dof]

    def planes_of(group):
        return [coef_ref[group * dof + k] for k in range(dof)]

    def body(m, carry):
        start = pl.multiple_of(m * per, per)
        at = [pl.ds(pl.multiple_of(start + k * rows, rows), rows) for k in range(dof)]
        row_ghost = jnp.where(last_row, down_ref[pl.ds(m, 1), :], up_ref[pl.ds(m, 1), :])
        col_ghost = roll(rim, -2 * m, 1)
        col_ghost2 = roll(rim2, -2 * m, 1)
        row_rim, col_rim, row_inv, col_inv = (planes_of(i) for i in range(4, 8))
        q = [qp_ref[at[k], :] + (row_rim[k] * row_ghost + col_rim[k] * col_ghost) for k in range(dof)]
        g = [gp_ref[at[k], :] + (row_inv[k] * row_ghost + col_inv[k] * col_ghost) for k in range(dof)]
        span, span_b, chord, chord_b = (planes_of(i) for i in range(4))
        fwd_s, bwd_s, fwd_c, bwd_c = dot(span, g), dot(span_b, g), dot(chord, g), dot(chord_b, g)
        near = [
            jnp.where(last_row, down2_ref[pl.ds(m, 1), :], roll(bwd_s, -1, 0)),
            jnp.where(first_row, up2_ref[pl.ds(m, 1), :], roll(fwd_s, 1, 0)),
            jnp.where(last_col, col_ghost2, roll(bwd_c, -1, 1)),
            jnp.where(first_col, col_ghost2, roll(fwd_c, 1, 1)),
        ]
        q2 = [axpy4([span[k], span_b[k], chord[k], chord_b[k]], near) for k in range(dof)]
        z = [z_ref[at[k], :] for k in range(dof)]
        load = [load_ref[at[k], :] for k in range(dof)]
        for which, (left, right) in enumerate(((z, load), (z, q), (g, q), (g, q2))):
            spot = pl.multiple_of((which * modes + m) * rows, rows)
            sum_ref[pl.ds(spot, rows), :] = dot(left, right)
        for k in range(dof):
            q_ref[at[k], :] = q[k]
            g_ref[at[k], :] = g[k]
            q2_ref[at[k], :] = q2[k]
        corners = (
            jnp.where(last_row, fwd_s, bwd_s),
            jnp.where(last_col, fwd_c, bwd_c),
            corner_kappa * col_ghost,
            corner_kappa * row_ghost,
        )
        mine = (lane >> 1) == m
        return tuple(jnp.where(mine, roll(new, 2 * m + 1, 1), old) for new, old in zip(corners, carry))

    corners = lax.fori_loop(0, modes, body, (zero,) * 4)
    sums = []
    for block in range(4 * modes // 8):
        base = block * 8 * rows
        total = sum_ref[pl.ds(base, 8, stride=rows), :]
        for r in range(1, rows):
            total = total + sum_ref[pl.ds(base + r, 8, stride=rows), :]
        sums.append(total)
    sums = jnp.concatenate(sums, axis=0)
    sums = lax.dot_general(
        jnp.ones((8, cols), F32), sums, (((1,), (1,)), ((), ())),
        precision=lax.Precision.HIGHEST, preferred_element_type=F32,
    )
    chunk = jnp.where(first_row, sums[0:1], zero)
    for which, corner in enumerate(corners):
        line = jnp.where(lane < cols // 2, corner[0:1], roll(jnp.broadcast_to(corner[rows - 1:rows], (rows, cols)), cols // 2, 1))
        chunk = jnp.where(row == which + 1, line, chunk)

    def send(d, carry):
        chunk_ref[pl.ds(pl.multiple_of(d * rows, rows), rows), :] = chunk
        return carry

    lax.fori_loop(0, devices, send, 0)


def last_kernel(dims, sizes, steps, part_ref, coef_ref, load_ref, z_ref, q_ref, g_ref, q2_ref,
                adjoint_ref, residual_ref, a_ref, b_ref, fix_ref):
    modes, dof, rows, cols = dims
    slabs, subs = sizes
    devices = slabs * subs
    row, lane = tile_iota((rows, cols))
    per = dof * rows
    half = cols // 2

    @pl.when(pl.program_id(0) == 0)
    def scalars():
        def lines(which):
            return part_ref[pl.ds(which, devices, stride=8), :]

        own_row, own_col, miss_row, miss_col = (lines(i) for i in range(1, 5))
        wide = lax.broadcasted_iota(jnp.int32, (devices, cols), 1)
        swapped = roll(miss_row, half, 1)
        met_row = jnp.where(wide >= half, roll(swapped, -subs, 0), roll(swapped, subs, 0))
        met_col = jnp.where((wide & 1) == 0, roll(roll(miss_col, -1, 1), -1, 0), roll(roll(miss_col, 1, 1), 1, 0))
        total = jnp.sum(lines(0), axis=0, keepdims=True)
        missed = jnp.sum(own_row * met_row + own_col * met_col, axis=0, keepdims=True)
        big_row, big_lane = tile_iota((4 * modes, cols))
        spread = jnp.where(big_row == big_lane, total, 0.0)
        spread = spread + jnp.where(((big_lane & (half - 1)) >> 1) == big_row - 3 * modes, missed, 0.0)
        spread = lax.dot_general(
            spread, jnp.ones((cols, cols), F32), (((1,), (0,)), ((), ())),
            precision=lax.Precision.HIGHEST, preferred_element_type=F32,
        )
        m0, m1, m2, m3 = (spread[i * modes:(i + 1) * modes] for i in range(4))
        step0 = m0 / (m0 - m1)
        rest = 1.0 - step0
        rz1 = rest * rest * m0 + 2.0 * rest * step0 * m1 + step0 * step0 * m2
        c0 = rest + rz1 / m0
        pq1 = c0 * c0 * (m0 - m1) + 2.0 * c0 * step0 * (m1 - m2) + step0 * step0 * (m2 - m3)
        step1 = rz1 / pq1
        a_ref[...] = step0 + step1 * c0
        b_ref[...] = step1 * step0

        here = lax.axis_index("slab") * subs + lax.axis_index("sub")

        def line_of(device, which):
            device = lax.rem(device + devices, devices)
            line = part_ref[pl.ds(device * 8 + which, 1), :]
            return jnp.broadcast_to(line, (rows, cols))

        fix_ref[0:rows, :] = jnp.where(row == rows - 1, line_of(here + subs, 3), roll(line_of(here - subs, 3), half, 1))
        fix = jnp.where((lane & 1) == 0, roll(line_of(here + 1, 4), -1, 1), roll(line_of(here - 1, 4), 1, 1))
        fix_ref[rows:2 * rows, :] = jnp.where(row == rows - 1, roll(fix, half, 1), fix)

    corner = ((row == 0) | (row == rows - 1)) & ((lane == 0) | (lane == cols - 1))
    count = modes // steps

    def body(i, carry):
        m = pl.program_id(0) * count + i
        a = a_ref[pl.ds(m, 1), :]
        b = b_ref[pl.ds(m, 1), :]
        row_fix = b * jnp.where(corner, roll(fix_ref[0:rows, :], cols - 1 - 2 * m, 1), 0.0)
        col_fix = b * jnp.where(corner, roll(fix_ref[rows:2 * rows, :], cols - 1 - 2 * m, 1), 0.0)
        for k in range(dof):
            at = pl.ds(pl.multiple_of(i * per + k * rows, rows), rows)
            adjoint_ref[at, :] = a * z_ref[at, :] + b * g_ref[at, :]
            residual_ref[at, :] = (
                ((1.0 - a) * load_ref[at, :] + (a - b) * q_ref[at, :])
                + (b * q2_ref[at, :] + (coef_ref[4 * dof + k] * row_fix + coef_ref[5 * dof + k] * col_fix))
            )
        return carry

    lax.fori_loop(0, count, body, 0)


def body_of(sizes):
    slabs, subs = sizes
    devices = slabs * subs
    axes = ("slab", "sub")
    paths = [matching(slabs, subs, along, parity) for along in (True, False) for parity in (0, 1)]

    def exchange(arrays):
        return [lax.ppermute(array, axes, path) for array, path in zip(arrays, paths)]

    vmem = pl.BlockSpec(memory_space=pltpu.VMEM)
    smem = pl.BlockSpec(memory_space=pltpu.SMEM)
    params = pltpu.CompilerParams(vmem_limit_bytes=VMEM_LIMIT)

    def body(mode_shapes, span_stiff, chord_stiff, span_geo, chord_geo, ground, chord_len):
        modes, dof, rows, cols = mode_shapes.shape
        dims = mode_shapes.shape
        count = modes * dof * rows
        field = mode_shapes.reshape(count, cols)

        def call(kernel, name, inputs, specs, outs, scratch):
            return pl.pallas_call(
                kernel,
                out_shape=[jax.ShapeDtypeStruct(shape, F32) for shape in outs],
                in_specs=specs,
                out_specs=[vmem] * len(outs),
                scratch_shapes=[pltpu.VMEM(shape, F32) for shape in scratch],
                compiler_params=params,
                name=name,
            )(*inputs)

        row_shape, col_shape = (modes * dof + rows, cols), ((dof + 1) * rows, cols)
        rims = call(
            lambda *refs: pack_kernel(dims, *refs), "pack_rim",
            (field, span_stiff, chord_stiff, span_geo, chord_geo), [vmem] * 5,
            [row_shape, row_shape, col_shape, col_shape], [(count, cols)],
        )
        met = exchange(rims)
        full = (count, cols)
        row_shape, col_shape = (2 * modes + rows, cols), (3 * rows, cols)
        load, z, qp, gp, coef, *rims2 = call(
            lambda *refs: first_kernel(dims, sizes, *refs), "load_and_first",
            (field, span_stiff, chord_stiff, span_geo, chord_geo, ground, chord_len, *rims, *met),
            [vmem] * 6 + [smem] + [vmem] * 8,
            [full] * 4 + [(8 * dof + 1, rows, cols)] + [row_shape, row_shape, col_shape, col_shape],
            [(dof * (dof + 1) // 2, rows, cols), (modes, cols), (modes, cols), (modes * rows, cols), (modes * rows, cols)],
        )
        met2 = exchange(rims2)
        q, g, q2, chunk = call(
            lambda *refs: second_kernel(dims, devices, *refs), "second_and_sums",
            (load, z, qp, gp, coef, *rims2, *met2), [vmem] * 13,
            [full] * 3 + [(devices * 8, cols)],
            [(modes, cols)] * 4 + [(4 * modes * rows, cols)],
        )
        parts = lax.all_to_all(chunk.reshape(devices, 8, cols), axes, 0, 0).reshape(devices * 8, cols)
        steps = 4
        cut = pl.BlockSpec((count // steps, cols), lambda i: (i, 0))
        whole = lambda shape: pl.BlockSpec(shape, lambda i: (0,) * len(shape))
        adjoint, residual = pl.pallas_call(
            lambda *refs: last_kernel(dims, sizes, steps, *refs),
            grid=(steps,),
            out_shape=[jax.ShapeDtypeStruct(full, F32)] * 2,
            in_specs=[whole(parts.shape), whole(coef.shape)] + [cut] * 5,
            out_specs=[cut] * 2,
            scratch_shapes=[pltpu.VMEM((modes, cols), F32), pltpu.VMEM((modes, cols), F32), pltpu.VMEM((2 * rows, cols), F32)],
            compiler_params=params,
            name="combine",
        )(parts, coef, load, z, q, g, q2)
        return adjoint.reshape(dims), residual.reshape(dims)

    return body


def solution(mesh):
    return jax.shard_map(
        body_of((mesh.shape["slab"], mesh.shape["sub"])),
        mesh=mesh,
        in_specs=(
            P(None, None, "slab", "sub"),
            P(None, "slab", "sub"),
            P(None, "slab", "sub"),
            P("slab", "sub"),
            P("slab", "sub"),
            P(None, "slab", "sub"),
            P(),
        ),
        out_specs=(P(None, None, "slab", "sub"), P(None, None, "slab", "sub")),
        check_vma=False,
    )
```

```python
import jax
import jax.numpy as jnp
from jax import lax
from jax.experimental import pallas as pl
from jax.experimental.pallas import tpu as pltpu
from jax.sharding import PartitionSpec as P

F32 = jnp.float32
VMEM_LIMIT = 24 * 1024 * 1024
LINES = 4


def matching(slabs, subs, along_slab, parity):
    pairs = []
    for s in range(slabs):
        for c in range(subs):
            here, count = (s, slabs) if along_slab else (c, subs)
            there = here + 1 if here % 2 == parity else here - 1
            if 0 <= there < count:
                target = (there, c) if along_slab else (s, there)
            elif along_slab:
                target = (s, c ^ 1) if subs % 2 == 0 else None
            else:
                target = (s, subs - 1 - c) if subs % 2 == 0 else None
            if target is not None:
                pairs.append((s * subs + c, target[0] * subs + target[1]))
    return pairs


def roll(value, shift, axis):
    size = value.shape[axis]
    if isinstance(shift, int):
        return pltpu.roll(value, shift % size, axis)
    return pltpu.roll(value, lax.rem(shift + size, size), axis)


def dot(left, right):
    total = left[0] * right[0]
    for k in range(1, len(left)):
        total = total + left[k] * right[k]
    return total


def axpy4(coefs, values):
    total = coefs[0] * values[0]
    for k in range(1, len(coefs)):
        total = total + coefs[k] * values[k]
    return total


def tile_iota(shape):
    return lax.broadcasted_iota(jnp.int32, shape, 0), lax.broadcasted_iota(jnp.int32, shape, 1)


def parities():
    return lax.rem(lax.axis_index("slab"), 2) == 0, lax.rem(lax.axis_index("sub"), 2) == 0


def pack_kernel(dims, sizes, parts, modes_hbm, span_hbm, chord_hbm, span_geo_hbm, chord_geo_hbm, len_hbm,
                field, live_ref, span_ref, chord_ref, span_geo_ref, chord_geo_ref, row_even, row_odd, col_even, col_odd,
                raw, len_ref, sems):
    modes, dof, rows, cols = dims
    row, lane = tile_iota((rows, cols))
    slab_even, sub_even = parities()
    per = dof * rows
    share = modes // parts
    fetches = [
        pltpu.make_async_copy(modes_hbm.at[pl.ds(i * share * per, share * per), :],
                              raw.at[pl.ds(i * share * per, share * per), :], sems.at[i])
        for i in range(parts)
    ]
    small = ((span_hbm, span_ref), (chord_hbm, chord_ref), (span_geo_hbm, span_geo_ref), (chord_geo_hbm, chord_geo_ref),
             (len_hbm, len_ref))
    others = [pltpu.make_async_copy(src, dst, sems.at[parts + i]) for i, (src, dst) in enumerate(small)]
    for copy in others + fetches:
        copy.start()
    for copy in others:
        copy.wait()

    stations = sizes[0] * rows
    row_start = lax.axis_index("slab") * rows
    col_start = lax.axis_index("sub") * cols

    def length(index):
        value = len_ref[jnp.clip(index, 0, stations - 1)]
        return jnp.where((index >= 0) & (index < stations), value, 0)

    lengths = [length(row_start + r) for r in range(-1, rows + 1)]
    own = jnp.zeros((rows, cols), jnp.int32)
    ahead = jnp.zeros((rows, cols), jnp.int32)
    for r in range(rows):
        own = jnp.where(row == r, lengths[r + 1], own)
        ahead = jnp.where(row == r, lengths[r + 2], ahead)
    column = col_start + lane
    up_live = (column < lengths[0]) & (column < lengths[1])
    left_live = (col_start < own) & (col_start > 0)
    live = ((column < own) & (column < ahead), column + 1 < own, up_live, left_live)
    for i, flags in enumerate(live):
        live_ref[i] = flags.astype(F32)

    packed = [jnp.zeros((rows, cols), F32) for k in range(dof)]
    for m in range(modes):
        if m % share == 0:
            fetches[m // share].wait()
        block = raw[m * per:(m + 1) * per, :].astype(F32)
        field[m * per:(m + 1) * per, :] = block
        mine = (lane >> 1) == m
        for k in range(dof):
            packed[k] = jnp.where(mine, roll(block[k * rows:(k + 1) * rows], 2 * m + 1, 1), packed[k])
        if m % 8 == 7:
            for k in range(dof):
                base = (m - 7) * per + k * rows
                first = field[pl.ds(base, 8, stride=per), :]
                last = field[pl.ds(base + rows - 1, 8, stride=per), :]
                out = k * modes + m - 7
                row_even[out:out + 8, :] = jnp.where(slab_even, last, first)
                row_odd[out:out + 8, :] = jnp.where(slab_even, first, last)
    field[modes * per:modes * per + rows, :] = jnp.zeros((rows, cols), F32)
    coef = jnp.zeros((rows, cols), F32)
    edge = jnp.zeros((rows, cols), F32)
    for k in range(dof + 1):
        span_plane = span_ref[k] if k < dof else span_geo_ref[...]
        chord_plane = chord_ref[k] if k < dof else chord_geo_ref[...]
        coef = jnp.where(row == k, span_plane[rows - 1:rows], coef)
        edge = jnp.where(lane == 2 * k, roll(chord_plane, 2 * k + 1, 1), edge)
    for k in range(dof):
        behind = roll(packed[k], -1, 1)
        col_even[k * rows:(k + 1) * rows, :] = jnp.where(sub_even, packed[k], behind)
        col_odd[k * rows:(k + 1) * rows, :] = jnp.where(sub_even, behind, packed[k])
    row_even[dof * modes:dof * modes + rows, :] = coef
    row_odd[dof * modes:dof * modes + rows, :] = coef
    col_even[dof * rows:(dof + 1) * rows, :] = edge
    col_odd[dof * rows:(dof + 1) * rows, :] = edge


def factor_blocks(blocks):
    count = len(blocks)
    factor = [[None] * count for i in range(count)]
    inverse = [None] * count
    for j in range(count):
        running = blocks[j][j]
        for k in range(j):
            running = running - factor[j][k] * factor[j][k]
        diag_root = jnp.sqrt(running)
        factor[j][j] = diag_root
        inverse[j] = 1.0 / diag_root
        for i in range(j + 1, count):
            running = blocks[i][j]
            for k in range(j):
                running = running - factor[i][k] * factor[j][k]
            factor[i][j] = running * inverse[j]
    return (factor, inverse)


def invert_blocks(blocks):
    count = len(blocks)
    factor, inverse = factor_blocks(blocks)
    lower = [[None] * count for i in range(count)]
    for j in range(count):
        lower[j][j] = inverse[j]
        for i in range(j + 1, count):
            running = factor[i][j] * lower[j][j]
            for k in range(j + 1, i):
                running = running + factor[i][k] * lower[k][j]
            lower[i][j] = -(running * inverse[i])
    result = [[None] * count for i in range(count)]
    for i in range(count):
        for j in range(i + 1):
            running = lower[i][i] * lower[i][j]
            for k in range(i + 1, count):
                running = running + lower[k][i] * lower[k][j]
            result[i][j] = running
    return result


def apply_inverse(entry, vector):
    count = len(vector)
    return [dot([entry(max(i, j), min(i, j)) for j in range(count)], vector) for i in range(count)]


def first_kernel(dims, modes_ref, live_ref, span_ref, chord_ref, span_geo_ref, chord_geo_ref, ground_ref,
                 row_even_out, row_odd_out, col_even_out, col_odd_out,
                 row_even_in, row_odd_in, col_even_in, col_odd_in,
                 load_ref, z_ref, q_ref, g_ref, coef_ref, row_even, row_odd, col_even, col_odd,
                 inv_ref, up_ref, down_ref, rim_ref, rim2_ref):
    modes, dof, rows, cols = dims
    row, lane = tile_iota((rows, cols))
    slab_even, sub_even = parities()
    per = dof * rows
    span_live, chord_live, up_live, left_live = (live_ref[i] > 0.0 for i in range(4))

    def row_weight(arrived, sent):
        total = None
        for k in range(dof):
            jump = arrived[k * modes:(k + 1) * modes, :] - sent[k * modes:(k + 1) * modes, :]
            total = jump * jump if total is None else total + jump * jump
        return total

    def col_weight(arrived, sent):
        total = None
        for k in range(dof):
            jump = arrived[k * rows:(k + 1) * rows, :] - sent[k * rows:(k + 1) * rows, :]
            total = jump * jump if total is None else total + jump * jump
        return total

    even_weight = row_weight(row_even_in, row_even_out)
    odd_weight = row_weight(row_odd_in, row_odd_out)
    up_weight = jnp.where(slab_even, odd_weight, even_weight)
    down_weight = jnp.where(slab_even, even_weight, odd_weight)
    tail = dof * modes
    up_coef = jnp.where(slab_even, row_odd_in[tail:tail + rows, :], row_even_in[tail:tail + rows, :])
    up_ref[...] = jnp.where(live_ref[2, 0:1, :] > 0.0, up_weight * up_coef[dof:dof + 1], 0.0)
    down_ref[...] = jnp.where(live_ref[0, rows - 1:rows, :] > 0.0, down_weight * span_geo_ref[rows - 1:rows, :], 0.0)
    even_col = col_weight(col_even_in, col_even_out)
    odd_col = col_weight(col_odd_in, col_odd_out)
    left_coef = jnp.where(sub_even, col_odd_in[per:per + rows, :], col_even_in[per:per + rows, :])
    left_weight = jnp.where(sub_even, odd_col, even_col) * left_coef[:, 2 * dof:2 * dof + 1]
    right_weight = jnp.where(sub_even, even_col, odd_col) * chord_geo_ref[:, cols - 1:cols]
    left_weight = jnp.where(left_live, left_weight, 0.0)
    right_weight = jnp.where(live_ref[1, :, cols - 1:cols] > 0.0, right_weight, 0.0)
    lane_even = (lane & 1) == 0
    rim_weight = jnp.where(lane_even, left_weight, roll(right_weight, -1, 1))

    first_row, last_row = row == 0, row == rows - 1
    first_col, last_col = lane == 0, lane == cols - 1

    zero = jnp.zeros((rows, cols), F32)
    span, span_b, chord, chord_b = [], [], [], []
    for k in range(dof):
        span.append(jnp.where(span_live, span_ref[k], zero))
        up = jnp.where(up_live, up_coef[k:k + 1], zero)
        span_b.append(jnp.where(first_row, up, roll(span[k], 1, 0)))
        chord.append(jnp.where(chord_live, chord_ref[k], zero))
        left = jnp.where(left_live, left_coef[:, 2 * k:2 * k + 1], zero)
        chord_b.append(jnp.where(first_col, left, roll(chord[k], 1, 1)))
    blocks = [[None] * dof for i in range(dof)]
    for i in range(dof):
        for j in range(i + 1):
            entry = span[i] * span[j] + span_b[i] * span_b[j] + chord[i] * chord[j] + chord_b[i] * chord_b[j]
            blocks[i][j] = entry + ground_ref[i] if i == j else entry
    inv = invert_blocks(blocks)
    place = {}
    for i in range(dof):
        for j in range(i + 1):
            place[i, j] = len(place)
            inv_ref[place[i, j]] = inv[i][j]
    row_rim = [jnp.where(last_row, span[k], jnp.where(first_row, span_b[k], zero)) for k in range(dof)]
    col_rim = [jnp.where(last_col, chord[k], jnp.where(first_col, chord_b[k], zero)) for k in range(dof)]
    row_inv = apply_inverse(lambda i, j: inv[i][j], row_rim)
    col_inv = apply_inverse(lambda i, j: inv[i][j], col_rim)
    for group, planes in enumerate((span, span_b, chord, chord_b, row_rim, col_rim, row_inv, col_inv)):
        for k in range(dof):
            coef_ref[group * dof + k] = planes[k]
    row_kappa = dot(row_rim, row_inv)
    col_kappa = dot(col_rim, col_inv)
    coef_ref[8 * dof] = dot(row_rim, col_inv)

    def planes_of(group):
        return [coef_ref[group * dof + k] for k in range(dof)]

    def body(m, carry):
        start = m * per
        v = [modes_ref[pl.ds(start + k * rows, rows), :] for k in range(dof)]
        down = down_ref[pl.ds(m, 1), :]
        up = up_ref[pl.ds(m, 1), :]
        rim = roll(rim_weight, -2 * m, 1)
        jumps = [modes_ref[pl.ds(start + k * rows + 1, rows), :] - v[k] for k in range(dof)]
        span_w = jnp.where(last_row, down, dot(jumps, jumps) * span_geo_ref[...])
        jumps = [roll(v[k], -1, 1) - v[k] for k in range(dof)]
        chord_w = jnp.where(last_col, rim, dot(jumps, jumps) * chord_geo_ref[...])
        span_wb = jnp.where(first_row, up, roll(span_w, 1, 0))
        chord_wb = jnp.where(first_col, rim, roll(chord_w, 1, 1))
        span, span_b, chord, chord_b = (planes_of(i) for i in range(4))
        load = [
            (span_b[k] * span_wb - span[k] * span_w) + (chord_b[k] * chord_wb - chord[k] * chord_w)
            for k in range(dof)
        ]
        entry = lambda i, j: inv_ref[place[i, j]]
        z = apply_inverse(entry, load)
        fwd_s, bwd_s, fwd_c, bwd_c = dot(span, z), dot(span_b, z), dot(chord, z), dot(chord_b, z)
        near = [
            jnp.where(last_row, zero, roll(bwd_s, -1, 0)),
            jnp.where(first_row, zero, roll(fwd_s, 1, 0)),
            jnp.where(last_col, zero, roll(bwd_c, -1, 1)),
            jnp.where(first_col, zero, roll(fwd_c, 1, 1)),
        ]
        q = [axpy4([span[k], span_b[k], chord[k], chord_b[k]], near) for k in range(dof)]
        g = apply_inverse(entry, q)
        for k in range(dof):
            at = pl.ds(start + k * rows, rows)
            load_ref[at, :] = load[k]
            z_ref[at, :] = z[k]
            q_ref[at, :] = q[k]
            g_ref[at, :] = g[k]
        at = pl.ds(m * rows, rows)
        rim_ref[at, :] = jnp.where(last_row, fwd_s, bwd_s)
        rim2_ref[at, :] = dot(planes_of(4), g)
        mine = (lane >> 1) == m
        col_z = roll(jnp.where(last_col, fwd_c, bwd_c), 2 * m + 1, 1)
        col_g = roll(dot(planes_of(5), g), 2 * m + 1, 1)
        return jnp.where(mine, col_z, carry[0]), jnp.where(mine, col_g, carry[1])

    col_z, col_g = zero, zero
    for m in range(modes):
        col_z, col_g = body(m, (col_z, col_g))
    for which, packed in enumerate((col_z, col_g, roll(col_kappa, 1, 1))):
        behind = roll(packed, -1, 1)
        col_even[which * rows:(which + 1) * rows, :] = jnp.where(sub_even, packed, behind)
        col_odd[which * rows:(which + 1) * rows, :] = jnp.where(sub_even, behind, packed)
    for which, ref in enumerate((rim_ref, rim2_ref)):
        for block in range(modes // 8):
            first = ref[pl.ds(block * 8 * rows, 8, stride=rows), :]
            last = ref[pl.ds(block * 8 * rows + rows - 1, 8, stride=rows), :]
            out = which * modes + block * 8
            row_even[out:out + 8, :] = jnp.where(slab_even, last, first)
            row_odd[out:out + 8, :] = jnp.where(slab_even, first, last)
    first = jnp.where(first_row, row_kappa[0:1], zero)
    last = jnp.where(first_row, row_kappa[rows - 1:rows], zero)
    row_even[2 * modes:2 * modes + rows, :] = jnp.where(slab_even, last, first)
    row_odd[2 * modes:2 * modes + rows, :] = jnp.where(slab_even, first, last)


def second_kernel(dims, devices, load_ref, z_ref, qp_ref, gp_ref, coef_ref,
                  row_even_out, row_odd_out, col_even_out, col_odd_out,
                  row_even_in, row_odd_in, col_even_in, col_odd_in,
                  q_ref, g_ref, q2_ref, chunk_ref,
                  up_ref, down_ref, up2_ref, down2_ref, sum_ref):
    modes, dof, rows, cols = dims
    row, lane = tile_iota((rows, cols))
    slab_even, sub_even = parities()
    per = dof * rows
    first_row, last_row = row == 0, row == rows - 1
    first_col, last_col = lane == 0, lane == cols - 1
    lane_even = (lane & 1) == 0
    zero = jnp.zeros((rows, cols), F32)

    def pick(flag, even, odd, start, size):
        return jnp.where(flag, even[start:start + size, :], odd[start:start + size, :])

    up_flag = jnp.logical_not(slab_even)
    left_flag = jnp.logical_not(sub_even)
    up_ref[...] = pick(up_flag, row_even_in, row_odd_in, 0, modes)
    down_ref[...] = pick(slab_even, row_even_in, row_odd_in, 0, modes)
    up2_ref[...] = (
        pick(up_flag, row_even_in, row_odd_in, modes, modes)
        + pick(up_flag, row_even_in, row_odd_in, 2 * modes, 1) * pick(up_flag, row_even_out, row_odd_out, 0, modes)
    )
    down2_ref[...] = (
        pick(slab_even, row_even_in, row_odd_in, modes, modes)
        + pick(slab_even, row_even_in, row_odd_in, 2 * modes, 1) * pick(slab_even, row_even_out, row_odd_out, 0, modes)
    )

    def merge(left, right):
        return jnp.where(lane_even, left, roll(right, -1, 1))

    def second_col(flag):
        kappa = pick(flag, col_even_in, col_odd_in, 2 * rows, rows)[:, 0:1]
        return pick(flag, col_even_in, col_odd_in, rows, rows) + kappa * pick(flag, col_even_out, col_odd_out, 0, rows)

    rim = merge(pick(left_flag, col_even_in, col_odd_in, 0, rows), pick(sub_even, col_even_in, col_odd_in, 0, rows))
    rim2 = merge(second_col(left_flag), second_col(sub_even))
    corner_kappa = coef_ref[8 * dof]

    def planes_of(group):
        return [coef_ref[group * dof + k] for k in range(dof)]

    def body(m, carry):
        start = m * per
        at = [pl.ds(start + k * rows, rows) for k in range(dof)]
        row_ghost = jnp.where(last_row, down_ref[pl.ds(m, 1), :], up_ref[pl.ds(m, 1), :])
        col_ghost = roll(rim, -2 * m, 1)
        col_ghost2 = roll(rim2, -2 * m, 1)
        row_rim, col_rim, row_inv, col_inv = (planes_of(i) for i in range(4, 8))
        q = [qp_ref[at[k], :] + (row_rim[k] * row_ghost + col_rim[k] * col_ghost) for k in range(dof)]
        g = [gp_ref[at[k], :] + (row_inv[k] * row_ghost + col_inv[k] * col_ghost) for k in range(dof)]
        span, span_b, chord, chord_b = (planes_of(i) for i in range(4))
        fwd_s, bwd_s, fwd_c, bwd_c = dot(span, g), dot(span_b, g), dot(chord, g), dot(chord_b, g)
        near = [
            jnp.where(last_row, down2_ref[pl.ds(m, 1), :], roll(bwd_s, -1, 0)),
            jnp.where(first_row, up2_ref[pl.ds(m, 1), :], roll(fwd_s, 1, 0)),
            jnp.where(last_col, col_ghost2, roll(bwd_c, -1, 1)),
            jnp.where(first_col, col_ghost2, roll(fwd_c, 1, 1)),
        ]
        q2 = [axpy4([span[k], span_b[k], chord[k], chord_b[k]], near) for k in range(dof)]
        z = [z_ref[at[k], :] for k in range(dof)]
        load = [load_ref[at[k], :] for k in range(dof)]
        miss = (corner_kappa * col_ghost, corner_kappa * row_ghost)
        cross = miss[0] * jnp.where(last_row, near[0], near[1]) + miss[1] * jnp.where(last_col, near[2], near[3])
        for which, (left, right) in enumerate(((z, load), (z, q), (g, q), (g, q2))):
            spot = (which * modes + m) * rows
            total = dot(left, right)
            sum_ref[pl.ds(spot, rows), :] = total + cross if which == 3 else total
        for k in range(dof):
            q_ref[at[k], :] = q[k]
            g_ref[at[k], :] = g[k]
            q2_ref[at[k], :] = q2[k]
        mine = (lane >> 1) == m
        return tuple(jnp.where(mine, roll(new, 2 * m + 1, 1), old) for new, old in zip(miss, carry))

    corners = (zero, zero)
    for m in range(modes):
        corners = body(m, corners)
    sums = []
    for block in range(4 * modes // 8):
        base = block * 8 * rows
        total = sum_ref[pl.ds(base, 8, stride=rows), :]
        for r in range(1, rows):
            total = total + sum_ref[pl.ds(base + r, 8, stride=rows), :]
        sums.append(total)
    sums = jnp.concatenate(sums, axis=0)
    sums = lax.dot_general(
        jnp.ones((8, cols), F32), sums, (((1,), (1,)), ((), ())),
        precision=lax.Precision.HIGHEST, preferred_element_type=F32,
    )
    chunk = jnp.where(row % LINES == 0, sums[0:1], zero)
    for which, corner in enumerate(corners):
        far = roll(jnp.broadcast_to(corner[rows - 1:rows], (rows, cols)), cols // 2, 1)
        line = jnp.where(lane < cols // 2, corner[0:1], far)
        chunk = jnp.where(row % LINES == which + 1, line, chunk)

    def send(d, carry):
        chunk_ref[pl.ds(pl.multiple_of(d * rows, rows), rows), :] = chunk
        return carry

    lax.fori_loop(0, devices * LINES // rows, send, 0, unroll=8)


def last_kernel(dims, sizes, steps, part_ref, coef_ref, load_ref, z_ref, q_ref, g_ref, q2_ref,
                adjoint_hbm, residual_hbm, a_ref, b_ref, adjoint_ref, residual_ref, sems):
    modes, dof, rows, cols = dims
    slabs, subs = sizes
    devices = slabs * subs
    row, lane = tile_iota((rows, cols))
    per = dof * rows
    half = cols // 2

    def lines(which):
        return part_ref[pl.ds(which, devices, stride=LINES), :]

    miss_row, miss_col = lines(1), lines(2)
    wide = lax.broadcasted_iota(jnp.int32, (devices, cols), 1)
    swapped = roll(miss_row, half, 1)
    met_row = jnp.where(wide >= half, roll(swapped, -subs, 0), roll(swapped, subs, 0))
    met_col = jnp.where((wide & 1) == 0, roll(roll(miss_col, -1, 1), -1, 0), roll(roll(miss_col, 1, 1), 1, 0))
    total = jnp.sum(lines(0), axis=0, keepdims=True)
    missed = jnp.sum(miss_row * met_row + miss_col * met_col, axis=0, keepdims=True)
    big_row, big_lane = tile_iota((4 * modes, cols))
    spread = jnp.where(big_row == big_lane, total, 0.0)
    spread = spread + jnp.where(((big_lane & (half - 1)) >> 1) == big_row - 3 * modes, missed, 0.0)
    spread = lax.dot_general(
        spread, jnp.ones((cols, cols), F32), (((1,), (0,)), ((), ())),
        precision=lax.Precision.HIGHEST, preferred_element_type=F32,
    )
    m0, m1, m2, m3 = (spread[i * modes:(i + 1) * modes] for i in range(4))
    step0 = m0 / (m0 - m1)
    rest = 1.0 - step0
    rz1 = rest * rest * m0 + 2.0 * rest * step0 * m1 + step0 * step0 * m2
    c0 = rest + rz1 / m0
    pq1 = c0 * c0 * (m0 - m1) + 2.0 * c0 * step0 * (m1 - m2) + step0 * step0 * (m2 - m3)
    step1 = rz1 / pq1
    a_ref[...] = step0 + step1 * c0
    b_ref[...] = step1 * step0

    here = lax.axis_index("slab") * subs + lax.axis_index("sub")

    def line_of(device, which):
        device = lax.rem(device + devices, devices)
        return jnp.broadcast_to(part_ref[pl.ds(device * LINES + which, 1), :], (rows, cols))

    row_fixes = jnp.where(row == rows - 1, line_of(here + subs, 1), roll(line_of(here - subs, 1), half, 1))
    col_fixes = jnp.where((lane & 1) == 0, roll(line_of(here + 1, 2), -1, 1), roll(line_of(here - 1, 2), 1, 1))
    col_fixes = jnp.where(row == rows - 1, roll(col_fixes, half, 1), col_fixes)
    corner = ((row == 0) | (row == rows - 1)) & ((lane == 0) | (lane == cols - 1))
    count = modes // steps
    copies = []
    for m in range(modes):
        a = a_ref[m:m + 1, :]
        b = b_ref[m:m + 1, :]
        row_fix = b * jnp.where(corner, roll(row_fixes, -1 - 2 * m, 1), 0.0)
        col_fix = b * jnp.where(corner, roll(col_fixes, -1 - 2 * m, 1), 0.0)
        for k in range(dof):
            at = pl.ds(m * per + k * rows, rows)
            adjoint_ref[at, :] = a * z_ref[at, :] + b * g_ref[at, :]
            residual_ref[at, :] = (
                ((1.0 - a) * load_ref[at, :] + (a - b) * q_ref[at, :])
                + (b * q2_ref[at, :] + (coef_ref[4 * dof + k] * row_fix + coef_ref[5 * dof + k] * col_fix))
            )
        if (m + 1) % count == 0:
            at = pl.ds((m + 1 - count) * per, count * per)
            for src, dst in ((adjoint_ref, adjoint_hbm), (residual_ref, residual_hbm)):
                copy = pltpu.make_async_copy(src.at[at, :], dst.at[at, :], sems.at[len(copies)])
                copy.start()
                copies.append(copy)
    for copy in copies:
        copy.wait()


def body_of(sizes):
    slabs, subs = sizes
    devices = slabs * subs
    axes = ("slab", "sub")
    paths = [matching(slabs, subs, along, parity) for along in (True, False) for parity in (0, 1)]

    def exchange(arrays):
        return [lax.ppermute(array, axes, path) for array, path in zip(arrays, paths)]

    vmem = pl.BlockSpec(memory_space=pltpu.VMEM)
    hbm = pl.BlockSpec(memory_space=pltpu.HBM)

    def body(mode_shapes, span_stiff, chord_stiff, span_geo, chord_geo, ground, chord_len):
        modes, dof, rows, cols = mode_shapes.shape
        dims = mode_shapes.shape
        count = modes * dof * rows

        def call(kernel, name, inputs, in_specs, outs, scratch, out_spec=vmem):
            return pl.pallas_call(
                kernel,
                out_shape=[jax.ShapeDtypeStruct(shape, F32) for shape in outs],
                in_specs=in_specs,
                out_specs=[out_spec] * len(outs),
                scratch_shapes=[pltpu.VMEM(s, F32) if isinstance(s, tuple) else s for s in scratch],
                compiler_params=pltpu.CompilerParams(vmem_limit_bytes=VMEM_LIMIT),
                name=name,
            )(*inputs)

        plane, planes, full = (rows, cols), (dof, rows, cols), (count, cols)
        row_shape, col_shape = (modes * dof + rows, cols), ((dof + 1) * rows, cols)
        parts = 4
        inputs = (mode_shapes.reshape(count, cols), span_stiff, chord_stiff, span_geo, chord_geo, chord_len)
        field, *coefs, row_even, row_odd, col_even, col_odd = call(
            lambda *refs: pack_kernel(dims, sizes, parts, *refs), "pack_rim",
            [pltpu.with_memory_space_constraint(x, pltpu.HBM) for x in inputs], [hbm] * 6,
            [(count + rows, cols), (4, rows, cols), planes, planes, plane, plane, row_shape, row_shape, col_shape, col_shape],
            [pltpu.VMEM(full, mode_shapes.dtype), pltpu.SMEM(chord_len.shape, jnp.int32), pltpu.SemaphoreType.DMA((parts + 5,))],
        )
        rims = [row_even, row_odd, col_even, col_odd]
        met = exchange(rims)
        row_shape, col_shape = (2 * modes + rows, cols), (3 * rows, cols)
        load, z, qp, gp, coef, *rims2 = call(
            lambda *refs: first_kernel(dims, *refs), "load_and_first",
            (field, *coefs, ground, *rims, *met), [vmem] * 15,
            [full] * 4 + [(8 * dof + 1, rows, cols), row_shape, row_shape, col_shape, col_shape],
            [(dof * (dof + 1) // 2, rows, cols), (modes, cols), (modes, cols), (modes * rows, cols), (modes * rows, cols)],
        )
        met2 = exchange(rims2)
        q, g, q2, chunk = call(
            lambda *refs: second_kernel(dims, devices, *refs), "second_and_sums",
            (load, z, qp, gp, coef, *rims2, *met2), [vmem] * 13,
            [full] * 3 + [(devices * LINES, cols)],
            [(modes, cols)] * 4 + [(4 * modes * rows, cols)],
        )
        shares = lax.all_to_all(chunk.reshape(devices, LINES, cols), axes, 0, 0).reshape(devices * LINES, cols)
        steps = 4
        adjoint, residual = call(
            lambda *refs: last_kernel(dims, sizes, steps, *refs), "combine",
            (shares, coef, load, z, q, g, q2), [vmem] * 7, [full] * 2,
            [(modes, cols), (modes, cols), full, full, pltpu.SemaphoreType.DMA((2 * steps,))], hbm,
        )
        return adjoint.reshape(dims), residual.reshape(dims)

    return body


def solution(mesh):
    return jax.shard_map(
        body_of((mesh.shape["slab"], mesh.shape["sub"])),
        mesh=mesh,
        in_specs=(
            P(None, None, "slab", "sub"),
            P(None, "slab", "sub"),
            P(None, "slab", "sub"),
            P("slab", "sub"),
            P("slab", "sub"),
            P(None, "slab", "sub"),
            P(),
        ),
        out_specs=(P(None, None, "slab", "sub"), P(None, None, "slab", "sub")),
        check_vma=False,
    )
```

```python
import jax
import jax.numpy as jnp
from jax import lax
from jax.experimental import pallas as pl
from jax.experimental.pallas import tpu as pltpu
from jax.sharding import PartitionSpec as P

F32 = jnp.float32
VMEM_LIMIT = 24 * 1024 * 1024
LINES = 4


def matching(slabs, subs, along_slab, parity):
    pairs = []
    for s in range(slabs):
        for c in range(subs):
            here, count = (s, slabs) if along_slab else (c, subs)
            there = here + 1 if here % 2 == parity else here - 1
            if 0 <= there < count:
                target = (there, c) if along_slab else (s, there)
            elif along_slab:
                target = (s, c ^ 1) if subs % 2 == 0 else None
            else:
                target = (s, subs - 1 - c) if subs % 2 == 0 else None
            if target is not None:
                pairs.append((s * subs + c, target[0] * subs + target[1]))
    return pairs


def roll(value, shift, axis):
    size = value.shape[axis]
    if isinstance(shift, int):
        return pltpu.roll(value, shift % size, axis)
    return pltpu.roll(value, lax.rem(shift + size, size), axis)


def dot(left, right):
    total = left[0] * right[0]
    for k in range(1, len(left)):
        total = total + left[k] * right[k]
    return total


def axpy4(coefs, values):
    total = coefs[0] * values[0]
    for k in range(1, len(coefs)):
        total = total + coefs[k] * values[k]
    return total


def tile_iota(shape):
    return lax.broadcasted_iota(jnp.int32, shape, 0), lax.broadcasted_iota(jnp.int32, shape, 1)


def parities():
    return lax.rem(lax.axis_index("slab"), 2) == 0, lax.rem(lax.axis_index("sub"), 2) == 0


def pack_kernel(dims, sizes, parts, modes_hbm, span_hbm, chord_hbm, span_geo_hbm, chord_geo_hbm, len_hbm,
                field, live_ref, span_ref, chord_ref, span_geo_ref, chord_geo_ref, row_even, row_odd, col_even, col_odd,
                raw, len_ref, sems):
    modes, dof, rows, cols = dims
    row, lane = tile_iota((rows, cols))
    slab_even, sub_even = parities()
    per = dof * rows
    share = modes // parts
    fetches = [
        pltpu.make_async_copy(modes_hbm.at[pl.ds(i * share * per, share * per), :],
                              raw.at[pl.ds(i * share * per, share * per), :], sems.at[i])
        for i in range(parts)
    ]
    small = ((span_hbm, span_ref), (chord_hbm, chord_ref), (span_geo_hbm, span_geo_ref), (chord_geo_hbm, chord_geo_ref),
             (len_hbm, len_ref))
    others = [pltpu.make_async_copy(src, dst, sems.at[parts + i]) for i, (src, dst) in enumerate(small)]
    for copy in others + fetches:
        copy.start()
    for copy in others:
        copy.wait()

    stations = sizes[0] * rows
    row_start = lax.axis_index("slab") * rows
    col_start = lax.axis_index("sub") * cols

    def length(index):
        value = len_ref[jnp.clip(index, 0, stations - 1)]
        return jnp.where((index >= 0) & (index < stations), value, 0)

    lengths = [length(row_start + r) for r in range(-1, rows + 1)]
    own = jnp.zeros((rows, cols), jnp.int32)
    ahead = jnp.zeros((rows, cols), jnp.int32)
    for r in range(rows):
        own = jnp.where(row == r, lengths[r + 1], own)
        ahead = jnp.where(row == r, lengths[r + 2], ahead)
    column = col_start + lane
    up_live = (column < lengths[0]) & (column < lengths[1])
    left_live = (col_start < own) & (col_start > 0)
    live = ((column < own) & (column < ahead), column + 1 < own, up_live, left_live)
    for i, flags in enumerate(live):
        live_ref[i] = flags.astype(F32)

    packed = [jnp.zeros((rows, cols), F32) for k in range(dof)]
    for m in range(modes):
        if m % share == 0:
            fetches[m // share].wait()
        block = raw[m * per:(m + 1) * per, :].astype(F32)
        field[m * per:(m + 1) * per, :] = block
        mine = (lane >> 1) == m
        for k in range(dof):
            packed[k] = jnp.where(mine, roll(block[k * rows:(k + 1) * rows], 2 * m + 1, 1), packed[k])
        if m % 8 == 7:
            for k in range(dof):
                base = (m - 7) * per + k * rows
                first = field[pl.ds(base, 8, stride=per), :]
                last = field[pl.ds(base + rows - 1, 8, stride=per), :]
                out = k * modes + m - 7
                row_even[out:out + 8, :] = jnp.where(slab_even, last, first)
                row_odd[out:out + 8, :] = jnp.where(slab_even, first, last)
    field[modes * per:modes * per + rows, :] = jnp.zeros((rows, cols), F32)
    coef = jnp.zeros((rows, cols), F32)
    edge = jnp.zeros((rows, cols), F32)
    for k in range(dof + 1):
        span_plane = span_ref[k] if k < dof else span_geo_ref[...]
        chord_plane = chord_ref[k] if k < dof else chord_geo_ref[...]
        coef = jnp.where(row == k, span_plane[rows - 1:rows], coef)
        edge = jnp.where(lane == 2 * k, roll(chord_plane, 2 * k + 1, 1), edge)
    for k in range(dof):
        behind = roll(packed[k], -1, 1)
        col_even[k * rows:(k + 1) * rows, :] = jnp.where(sub_even, packed[k], behind)
        col_odd[k * rows:(k + 1) * rows, :] = jnp.where(sub_even, behind, packed[k])
    row_even[dof * modes:dof * modes + rows, :] = coef
    row_odd[dof * modes:dof * modes + rows, :] = coef
    col_even[dof * rows:(dof + 1) * rows, :] = edge
    col_odd[dof * rows:(dof + 1) * rows, :] = edge


def invert_blocks(blocks):
    count = len(blocks)
    scaled = [[None] * count for i in range(count)]
    factor = [[None] * count for i in range(count)]
    inverse = [None] * count
    for j in range(count):
        running = blocks[j][j]
        for k in range(j):
            running = running - scaled[j][k] * factor[j][k]
        inverse[j] = 1.0 / running
        for i in range(j + 1, count):
            running = blocks[i][j]
            for k in range(j):
                running = running - scaled[i][k] * factor[j][k]
            scaled[i][j] = running
            factor[i][j] = running * inverse[j]
    lower = [[None] * count for i in range(count)]
    for j in range(count):
        for i in range(j + 1, count):
            running = factor[i][j]
            for k in range(j + 1, i):
                running = running + factor[i][k] * lower[k][j]
            lower[i][j] = -running
    result = [[None] * count for i in range(count)]
    for i in range(count):
        for j in range(i + 1):
            running = inverse[i] if i == j else inverse[i] * lower[i][j]
            for k in range(i + 1, count):
                running = running + (lower[k][i] * inverse[k]) * lower[k][j]
            result[i][j] = running
    return result


def times_ones(value, transposed):
    high = value.astype(jnp.bfloat16)
    rest = value - high.astype(F32)
    middle = rest.astype(jnp.bfloat16)
    low = (rest - middle.astype(F32)).astype(jnp.bfloat16)
    pieces = jnp.concatenate([high, middle, low], axis=1)
    if transposed:
        ones = jnp.ones((8, pieces.shape[1]), jnp.bfloat16)
        return lax.dot_general(ones, pieces, (((1,), (1,)), ((), ())), preferred_element_type=F32)
    ones = jnp.ones((pieces.shape[1], value.shape[1]), jnp.bfloat16)
    return lax.dot_general(pieces, ones, (((1,), (0,)), ((), ())), preferred_element_type=F32)


def inverse_place(dof, i, j):
    return 8 * dof + 1 + i * (i + 1) // 2 + j


def apply_inverse(entry, vector):
    count = len(vector)
    return [dot([entry(max(i, j), min(i, j)) for j in range(count)], vector) for i in range(count)]


def inner_kernel(dims, modes_ref, live_ref, span_ref, chord_ref, span_geo_ref, chord_geo_ref, load_ref):
    modes, dof, rows, cols = dims
    row, lane = tile_iota((rows, cols))
    per = dof * rows
    first_row, last_row = row == 0, row == rows - 1
    first_col, last_col = lane == 0, lane == cols - 1
    zero = jnp.zeros((rows, cols), F32)
    span_inner = (live_ref[0] > 0.0) & jnp.logical_not(last_row)
    chord_inner = (live_ref[1] > 0.0) & jnp.logical_not(last_col)
    span = [jnp.where(span_inner, span_ref[k], zero) for k in range(dof)]
    chord = [jnp.where(chord_inner, chord_ref[k], zero) for k in range(dof)]
    span_b = [jnp.where(first_row, zero, roll(span[k], 1, 0)) for k in range(dof)]
    chord_b = [jnp.where(first_col, zero, roll(chord[k], 1, 1)) for k in range(dof)]
    span_geo = jnp.where(span_inner, span_geo_ref[...], zero)
    chord_geo = jnp.where(chord_inner, chord_geo_ref[...], zero)
    for m in range(modes):
        start = m * per
        v = [modes_ref[pl.ds(start + k * rows, rows), :] for k in range(dof)]
        jumps = [modes_ref[pl.ds(start + k * rows + 1, rows), :] - v[k] for k in range(dof)]
        span_w = jnp.where(last_row, zero, dot(jumps, jumps) * span_geo)
        jumps = [roll(v[k], -1, 1) - v[k] for k in range(dof)]
        chord_w = jnp.where(last_col, zero, dot(jumps, jumps) * chord_geo)
        span_wb, chord_wb = roll(span_w, 1, 0), roll(chord_w, 1, 1)
        for k in range(dof):
            load_ref[pl.ds(start + k * rows, rows), :] = (
                (span_b[k] * span_wb - span[k] * span_w) + (chord_b[k] * chord_wb - chord[k] * chord_w)
            )


def first_kernel(dims, inner_ref, live_ref, span_ref, chord_ref, span_geo_ref, chord_geo_ref, ground_ref,
                 row_even_out, row_odd_out, col_even_out, col_odd_out,
                 row_even_in, row_odd_in, col_even_in, col_odd_in,
                 load_ref, z_ref, q_ref, coef_ref, row_even, row_odd, col_even, col_odd,
                 up_ref, down_ref, rim_ref, rim2_ref):
    modes, dof, rows, cols = dims
    row, lane = tile_iota((rows, cols))
    slab_even, sub_even = parities()
    per = dof * rows
    span_live, chord_live, up_live, left_live = (live_ref[i] > 0.0 for i in range(4))

    def row_weight(arrived, sent):
        total = None
        for k in range(dof):
            jump = arrived[k * modes:(k + 1) * modes, :] - sent[k * modes:(k + 1) * modes, :]
            total = jump * jump if total is None else total + jump * jump
        return total

    def col_weight(arrived, sent):
        total = None
        for k in range(dof):
            jump = arrived[k * rows:(k + 1) * rows, :] - sent[k * rows:(k + 1) * rows, :]
            total = jump * jump if total is None else total + jump * jump
        return total

    even_weight = row_weight(row_even_in, row_even_out)
    odd_weight = row_weight(row_odd_in, row_odd_out)
    up_weight = jnp.where(slab_even, odd_weight, even_weight)
    down_weight = jnp.where(slab_even, even_weight, odd_weight)
    tail = dof * modes
    up_coef = jnp.where(slab_even, row_odd_in[tail:tail + rows, :], row_even_in[tail:tail + rows, :])
    up_ref[...] = jnp.where(live_ref[2, 0:1, :] > 0.0, up_weight * up_coef[dof:dof + 1], 0.0)
    down_ref[...] = jnp.where(live_ref[0, rows - 1:rows, :] > 0.0, down_weight * span_geo_ref[rows - 1:rows, :], 0.0)
    even_col = col_weight(col_even_in, col_even_out)
    odd_col = col_weight(col_odd_in, col_odd_out)
    left_coef = jnp.where(sub_even, col_odd_in[per:per + rows, :], col_even_in[per:per + rows, :])
    left_weight = jnp.where(sub_even, odd_col, even_col) * left_coef[:, 2 * dof:2 * dof + 1]
    right_weight = jnp.where(sub_even, even_col, odd_col) * chord_geo_ref[:, cols - 1:cols]
    left_weight = jnp.where(left_live, left_weight, 0.0)
    right_weight = jnp.where(live_ref[1, :, cols - 1:cols] > 0.0, right_weight, 0.0)
    lane_even = (lane & 1) == 0
    rim_weight = jnp.where(lane_even, left_weight, roll(right_weight, -1, 1))

    first_row, last_row = row == 0, row == rows - 1
    first_col, last_col = lane == 0, lane == cols - 1

    zero = jnp.zeros((rows, cols), F32)
    span, span_b, chord, chord_b = [], [], [], []
    for k in range(dof):
        span.append(jnp.where(span_live, span_ref[k], zero))
        up = jnp.where(up_live, up_coef[k:k + 1], zero)
        span_b.append(jnp.where(first_row, up, roll(span[k], 1, 0)))
        chord.append(jnp.where(chord_live, chord_ref[k], zero))
        left = jnp.where(left_live, left_coef[:, 2 * k:2 * k + 1], zero)
        chord_b.append(jnp.where(first_col, left, roll(chord[k], 1, 1)))
    blocks = [[None] * dof for i in range(dof)]
    for i in range(dof):
        for j in range(i + 1):
            entry = span[i] * span[j] + span_b[i] * span_b[j] + chord[i] * chord[j] + chord_b[i] * chord_b[j]
            blocks[i][j] = entry + ground_ref[i] if i == j else entry
    inv = invert_blocks(blocks)
    for i in range(dof):
        for j in range(i + 1):
            coef_ref[inverse_place(dof, i, j)] = inv[i][j]
    row_rim = [jnp.where(last_row, span[k], jnp.where(first_row, span_b[k], zero)) for k in range(dof)]
    col_rim = [jnp.where(last_col, chord[k], jnp.where(first_col, chord_b[k], zero)) for k in range(dof)]
    row_sign = [jnp.where(last_row, -row_rim[k], row_rim[k]) for k in range(dof)]
    col_sign = [jnp.where(last_col, -col_rim[k], col_rim[k]) for k in range(dof)]
    row_inv = apply_inverse(lambda i, j: inv[i][j], row_rim)
    col_inv = apply_inverse(lambda i, j: inv[i][j], col_rim)
    for group, planes in enumerate((span, span_b, chord, chord_b, row_rim, col_rim, row_inv, col_inv)):
        for k in range(dof):
            coef_ref[group * dof + k] = planes[k]
    row_kappa = dot(row_rim, row_inv)
    col_kappa = dot(col_rim, col_inv)
    coef_ref[8 * dof] = dot(row_rim, col_inv)

    def planes_of(group):
        return [coef_ref[group * dof + k] for k in range(dof)]

    def body(m, carry):
        start = m * per
        row_w = jnp.where(last_row, down_ref[pl.ds(m, 1), :], up_ref[pl.ds(m, 1), :])
        col_w = roll(rim_weight, -2 * m, 1)
        span, span_b, chord, chord_b = (planes_of(i) for i in range(4))
        load = [
            inner_ref[pl.ds(start + k * rows, rows), :] + (row_sign[k] * row_w + col_sign[k] * col_w)
            for k in range(dof)
        ]
        z = apply_inverse(lambda i, j: coef_ref[inverse_place(dof, i, j)], load)
        fwd_s, bwd_s, fwd_c, bwd_c = dot(span, z), dot(span_b, z), dot(chord, z), dot(chord_b, z)
        near = [
            jnp.where(last_row, zero, roll(bwd_s, -1, 0)),
            jnp.where(first_row, zero, roll(fwd_s, 1, 0)),
            jnp.where(last_col, zero, roll(bwd_c, -1, 1)),
            jnp.where(first_col, zero, roll(fwd_c, 1, 1)),
        ]
        q = [axpy4([span[k], span_b[k], chord[k], chord_b[k]], near) for k in range(dof)]
        for k in range(dof):
            at = pl.ds(start + k * rows, rows)
            load_ref[at, :] = load[k]
            z_ref[at, :] = z[k]
            q_ref[at, :] = q[k]
        at = pl.ds(m * rows, rows)
        rim_ref[at, :] = jnp.where(last_row, fwd_s, bwd_s)
        rim2_ref[at, :] = dot(planes_of(6), q)
        mine = (lane >> 1) == m
        col_z = roll(jnp.where(last_col, fwd_c, bwd_c), 2 * m + 1, 1)
        col_g = roll(dot(planes_of(7), q), 2 * m + 1, 1)
        return jnp.where(mine, col_z, carry[0]), jnp.where(mine, col_g, carry[1])

    col_z, col_g = zero, zero
    for m in range(modes):
        col_z, col_g = body(m, (col_z, col_g))
    for which, packed in enumerate((col_z, col_g, roll(col_kappa, 1, 1))):
        behind = roll(packed, -1, 1)
        col_even[which * rows:(which + 1) * rows, :] = jnp.where(sub_even, packed, behind)
        col_odd[which * rows:(which + 1) * rows, :] = jnp.where(sub_even, behind, packed)
    for which, ref in enumerate((rim_ref, rim2_ref)):
        for block in range(modes // 8):
            first = ref[pl.ds(block * 8 * rows, 8, stride=rows), :]
            last = ref[pl.ds(block * 8 * rows + rows - 1, 8, stride=rows), :]
            out = which * modes + block * 8
            row_even[out:out + 8, :] = jnp.where(slab_even, last, first)
            row_odd[out:out + 8, :] = jnp.where(slab_even, first, last)
    first = jnp.where(first_row, row_kappa[0:1], zero)
    last = jnp.where(first_row, row_kappa[rows - 1:rows], zero)
    row_even[2 * modes:2 * modes + rows, :] = jnp.where(slab_even, last, first)
    row_odd[2 * modes:2 * modes + rows, :] = jnp.where(slab_even, first, last)


def solve_kernel(dims, load_ref, z_ref, q_ref, coef_ref, g_ref, first_ref, sum_ref):
    modes, dof, rows, cols = dims
    for m in range(modes):
        at = [pl.ds((m * dof + k) * rows, rows) for k in range(dof)]
        q = [q_ref[at[k], :] for k in range(dof)]
        g = apply_inverse(lambda i, j: coef_ref[inverse_place(dof, i, j)], q)
        for k in range(dof):
            g_ref[at[k], :] = g[k]
        z, load = [z_ref[at[k], :] for k in range(dof)], [load_ref[at[k], :] for k in range(dof)]
        sum_ref[pl.ds(m * rows, rows), :] = dot(z, load)
    for block in range(modes // 8):
        first_ref[block * 8:block * 8 + 8, :] = sum_of_rows(sum_ref, block * 8 * rows, rows)


def sum_of_rows(ref, base, rows):
    total = ref[pl.ds(base, 8, stride=rows), :]
    for r in range(1, rows):
        total = total + ref[pl.ds(base + r, 8, stride=rows), :]
    return total


def second_kernel(dims, devices, first_ref, z_ref, qp_ref, gp_ref, coef_ref,
                  row_even_out, row_odd_out, col_even_out, col_odd_out,
                  row_even_in, row_odd_in, col_even_in, col_odd_in,
                  q_ref, g_ref, q2_ref, chunk_ref,
                  up_ref, down_ref, up2_ref, down2_ref, sum_ref):
    modes, dof, rows, cols = dims
    row, lane = tile_iota((rows, cols))
    slab_even, sub_even = parities()
    per = dof * rows
    first_row, last_row = row == 0, row == rows - 1
    first_col, last_col = lane == 0, lane == cols - 1
    lane_even = (lane & 1) == 0
    zero = jnp.zeros((rows, cols), F32)

    def pick(flag, even, odd, start, size):
        return jnp.where(flag, even[start:start + size, :], odd[start:start + size, :])

    up_flag = jnp.logical_not(slab_even)
    left_flag = jnp.logical_not(sub_even)
    up_ref[...] = pick(up_flag, row_even_in, row_odd_in, 0, modes)
    down_ref[...] = pick(slab_even, row_even_in, row_odd_in, 0, modes)
    up2_ref[...] = (
        pick(up_flag, row_even_in, row_odd_in, modes, modes)
        + pick(up_flag, row_even_in, row_odd_in, 2 * modes, 1) * pick(up_flag, row_even_out, row_odd_out, 0, modes)
    )
    down2_ref[...] = (
        pick(slab_even, row_even_in, row_odd_in, modes, modes)
        + pick(slab_even, row_even_in, row_odd_in, 2 * modes, 1) * pick(slab_even, row_even_out, row_odd_out, 0, modes)
    )

    def merge(left, right):
        return jnp.where(lane_even, left, roll(right, -1, 1))

    def second_col(flag):
        kappa = pick(flag, col_even_in, col_odd_in, 2 * rows, rows)[:, 0:1]
        return pick(flag, col_even_in, col_odd_in, rows, rows) + kappa * pick(flag, col_even_out, col_odd_out, 0, rows)

    rim = merge(pick(left_flag, col_even_in, col_odd_in, 0, rows), pick(sub_even, col_even_in, col_odd_in, 0, rows))
    rim2 = merge(second_col(left_flag), second_col(sub_even))
    corner_kappa = coef_ref[8 * dof]

    def planes_of(group):
        return [coef_ref[group * dof + k] for k in range(dof)]

    def body(m, carry):
        start = m * per
        at = [pl.ds(start + k * rows, rows) for k in range(dof)]
        row_ghost = jnp.where(last_row, down_ref[pl.ds(m, 1), :], up_ref[pl.ds(m, 1), :])
        col_ghost = roll(rim, -2 * m, 1)
        col_ghost2 = roll(rim2, -2 * m, 1)
        row_rim, col_rim, row_inv, col_inv = (planes_of(i) for i in range(4, 8))
        q = [qp_ref[at[k], :] + (row_rim[k] * row_ghost + col_rim[k] * col_ghost) for k in range(dof)]
        g = [gp_ref[at[k], :] + (row_inv[k] * row_ghost + col_inv[k] * col_ghost) for k in range(dof)]
        span, span_b, chord, chord_b = (planes_of(i) for i in range(4))
        fwd_s, bwd_s, fwd_c, bwd_c = dot(span, g), dot(span_b, g), dot(chord, g), dot(chord_b, g)
        near = [
            jnp.where(last_row, down2_ref[pl.ds(m, 1), :], roll(bwd_s, -1, 0)),
            jnp.where(first_row, up2_ref[pl.ds(m, 1), :], roll(fwd_s, 1, 0)),
            jnp.where(last_col, col_ghost2, roll(bwd_c, -1, 1)),
            jnp.where(first_col, col_ghost2, roll(fwd_c, 1, 1)),
        ]
        q2 = [axpy4([span[k], span_b[k], chord[k], chord_b[k]], near) for k in range(dof)]
        z = [z_ref[at[k], :] for k in range(dof)]
        miss = (corner_kappa * col_ghost, corner_kappa * row_ghost)
        cross = miss[0] * jnp.where(last_row, near[0], near[1]) + miss[1] * jnp.where(last_col, near[2], near[3])
        for which, (left, right) in enumerate(((z, q), (g, q), (g, q2))):
            spot = (which * modes + m) * rows
            total = dot(left, right)
            sum_ref[pl.ds(spot, rows), :] = total + cross if which == 2 else total
        for k in range(dof):
            q_ref[at[k], :] = q[k]
            g_ref[at[k], :] = g[k]
            q2_ref[at[k], :] = q2[k]
        mine = (lane >> 1) == m
        return tuple(jnp.where(mine, roll(new, 2 * m + 1, 1), old) for new, old in zip(miss, carry))

    corners = (zero, zero)
    for m in range(modes):
        corners = body(m, corners)
    sums = [first_ref[...]] + [sum_of_rows(sum_ref, block * 8 * rows, rows) for block in range(3 * modes // 8)]
    sums = jnp.concatenate(sums, axis=0)
    sums = times_ones(sums, True)
    chunk = jnp.where(row % LINES == 0, sums[0:1], zero)
    for which, corner in enumerate(corners):
        far = roll(jnp.broadcast_to(corner[rows - 1:rows], (rows, cols)), cols // 2, 1)
        line = jnp.where(lane < cols // 2, corner[0:1], far)
        chunk = jnp.where(row % LINES == which + 1, line, chunk)

    def send(d, carry):
        chunk_ref[pl.ds(pl.multiple_of(d * rows, rows), rows), :] = chunk
        return carry

    lax.fori_loop(0, devices * LINES // rows, send, 0, unroll=8)


def last_kernel(dims, sizes, steps, part_ref, coef_ref, load_ref, z_ref, q_ref, g_ref, q2_ref,
                adjoint_hbm, residual_hbm, a_ref, b_ref, adjoint_ref, residual_ref, sems):
    modes, dof, rows, cols = dims
    slabs, subs = sizes
    devices = slabs * subs
    row, lane = tile_iota((rows, cols))
    per = dof * rows
    half = cols // 2

    def lines(which):
        return part_ref[pl.ds(which, devices, stride=LINES), :]

    miss_row, miss_col = lines(1), lines(2)
    wide = lax.broadcasted_iota(jnp.int32, (devices, cols), 1)
    swapped = roll(miss_row, half, 1)
    met_row = jnp.where(wide >= half, roll(swapped, -subs, 0), roll(swapped, subs, 0))
    met_col = jnp.where((wide & 1) == 0, roll(roll(miss_col, -1, 1), -1, 0), roll(roll(miss_col, 1, 1), 1, 0))
    total = jnp.sum(lines(0), axis=0, keepdims=True)
    missed = jnp.sum(miss_row * met_row + miss_col * met_col, axis=0, keepdims=True)
    big_row, big_lane = tile_iota((4 * modes, cols))
    spread = jnp.where(big_row == big_lane, total, 0.0)
    spread = spread + jnp.where(((big_lane & (half - 1)) >> 1) == big_row - 3 * modes, missed, 0.0)
    spread = times_ones(spread, False)
    m0, m1, m2, m3 = (spread[i * modes:(i + 1) * modes] for i in range(4))
    step0 = m0 / (m0 - m1)
    rest = 1.0 - step0
    rz1 = rest * rest * m0 + 2.0 * rest * step0 * m1 + step0 * step0 * m2
    c0 = rest + rz1 / m0
    pq1 = c0 * c0 * (m0 - m1) + 2.0 * c0 * step0 * (m1 - m2) + step0 * step0 * (m2 - m3)
    step1 = rz1 / pq1
    a_ref[...] = step0 + step1 * c0
    b_ref[...] = step1 * step0

    here = lax.axis_index("slab") * subs + lax.axis_index("sub")

    def line_of(device, which):
        device = lax.rem(device + devices, devices)
        return jnp.broadcast_to(part_ref[pl.ds(device * LINES + which, 1), :], (rows, cols))

    row_fixes = jnp.where(row == rows - 1, line_of(here + subs, 1), roll(line_of(here - subs, 1), half, 1))
    col_fixes = jnp.where((lane & 1) == 0, roll(line_of(here + 1, 2), -1, 1), roll(line_of(here - 1, 2), 1, 1))
    col_fixes = jnp.where(row == rows - 1, roll(col_fixes, half, 1), col_fixes)
    corner = ((row == 0) | (row == rows - 1)) & ((lane == 0) | (lane == cols - 1))
    count = modes // steps
    copies = []
    for m in range(modes):
        a = a_ref[m:m + 1, :]
        b = b_ref[m:m + 1, :]
        row_fix = b * jnp.where(corner, roll(row_fixes, -1 - 2 * m, 1), 0.0)
        col_fix = b * jnp.where(corner, roll(col_fixes, -1 - 2 * m, 1), 0.0)
        for k in range(dof):
            at = pl.ds(m * per + k * rows, rows)
            adjoint_ref[at, :] = a * z_ref[at, :] + b * g_ref[at, :]
            residual_ref[at, :] = (
                ((1.0 - a) * load_ref[at, :] + (a - b) * q_ref[at, :])
                + (b * q2_ref[at, :] + (coef_ref[4 * dof + k] * row_fix + coef_ref[5 * dof + k] * col_fix))
            )
        if (m + 1) % count == 0:
            at = pl.ds((m + 1 - count) * per, count * per)
            for src, dst in ((adjoint_ref, adjoint_hbm), (residual_ref, residual_hbm)):
                copy = pltpu.make_async_copy(src.at[at, :], dst.at[at, :], sems.at[len(copies)])
                copy.start()
                copies.append(copy)
    for copy in copies:
        copy.wait()


def body_of(sizes):
    slabs, subs = sizes
    devices = slabs * subs
    axes = ("slab", "sub")
    paths = [matching(slabs, subs, along, parity) for along in (True, False) for parity in (0, 1)]

    def exchange(arrays):
        return [lax.ppermute(array, axes, path) for array, path in zip(arrays, paths)]

    vmem = pl.BlockSpec(memory_space=pltpu.VMEM)
    hbm = pl.BlockSpec(memory_space=pltpu.HBM)

    def body(mode_shapes, span_stiff, chord_stiff, span_geo, chord_geo, ground, chord_len):
        modes, dof, rows, cols = mode_shapes.shape
        dims = mode_shapes.shape
        count = modes * dof * rows

        def call(kernel, name, inputs, in_specs, outs, scratch, out_spec=vmem):
            return pl.pallas_call(
                kernel,
                out_shape=[jax.ShapeDtypeStruct(shape, F32) for shape in outs],
                in_specs=in_specs,
                out_specs=[out_spec] * len(outs),
                scratch_shapes=[pltpu.VMEM(s, F32) if isinstance(s, tuple) else s for s in scratch],
                compiler_params=pltpu.CompilerParams(vmem_limit_bytes=VMEM_LIMIT),
                name=name,
            )(*inputs)

        plane, planes, full = (rows, cols), (dof, rows, cols), (count, cols)
        row_shape, col_shape = (modes * dof + rows, cols), ((dof + 1) * rows, cols)
        parts = 2
        inputs = (mode_shapes.reshape(count, cols), span_stiff, chord_stiff, span_geo, chord_geo, chord_len)
        field, *coefs, row_even, row_odd, col_even, col_odd = call(
            lambda *refs: pack_kernel(dims, sizes, parts, *refs), "pack_rim",
            [pltpu.with_memory_space_constraint(x, pltpu.HBM) for x in inputs], [hbm] * 6,
            [(count + rows, cols), (4, rows, cols), planes, planes, plane, plane, row_shape, row_shape, col_shape, col_shape],
            [pltpu.VMEM(full, mode_shapes.dtype), pltpu.SMEM(chord_len.shape, jnp.int32), pltpu.SemaphoreType.DMA((parts + 5,))],
        )
        rims = [row_even, row_odd, col_even, col_odd]
        met = exchange(rims)
        (inner,) = call(
            lambda *refs: inner_kernel(dims, *refs), "inner_load", (field, *coefs), [vmem] * 6, [full], [],
        )
        row_shape, col_shape = (2 * modes + rows, cols), (3 * rows, cols)
        load, z, qp, coef, *rims2 = call(
            lambda *refs: first_kernel(dims, *refs), "load_and_first",
            (inner, *coefs, ground, *rims, *met), [vmem] * 15,
            [full] * 3 + [(inverse_place(dof, dof, 0), rows, cols), row_shape, row_shape, col_shape, col_shape],
            [(modes, cols), (modes, cols), (modes * rows, cols), (modes * rows, cols)],
        )
        met2 = exchange(rims2)
        gp, first = call(
            lambda *refs: solve_kernel(dims, *refs), "solve_inner", (load, z, qp, coef), [vmem] * 4,
            [full, (modes, cols)], [(modes * rows, cols)],
        )
        q, g, q2, chunk = call(
            lambda *refs: second_kernel(dims, devices, *refs), "second_and_sums",
            (first, z, qp, gp, coef, *rims2, *met2), [vmem] * 13,
            [full] * 3 + [(devices * LINES, cols)],
            [(modes, cols)] * 4 + [(3 * modes * rows, cols)],
        )
        shares = lax.all_to_all(chunk.reshape(devices, LINES, cols), axes, 0, 0).reshape(devices * LINES, cols)
        steps = 4
        adjoint, residual = call(
            lambda *refs: last_kernel(dims, sizes, steps, *refs), "combine",
            (shares, coef, load, z, q, g, q2), [vmem] * 7, [full] * 2,
            [(modes, cols), (modes, cols), full, full, pltpu.SemaphoreType.DMA((2 * steps,))], hbm,
        )
        return adjoint.reshape(dims), residual.reshape(dims)

    return body


def solution(mesh):
    return jax.shard_map(
        body_of((mesh.shape["slab"], mesh.shape["sub"])),
        mesh=mesh,
        in_specs=(
            P(None, None, "slab", "sub"),
            P(None, "slab", "sub"),
            P(None, "slab", "sub"),
            P("slab", "sub"),
            P("slab", "sub"),
            P(None, "slab", "sub"),
            P(),
        ),
        out_specs=(P(None, None, "slab", "sub"), P(None, None, "slab", "sub")),
        check_vma=False,
    )
```

```python
import jax
import jax.numpy as jnp
from jax import lax
from jax.experimental import pallas as pl
from jax.experimental.pallas import tpu as pltpu
from jax.sharding import PartitionSpec as P

F32 = jnp.float32
VMEM_LIMIT = 24 * 1024 * 1024
LINES = 4


def matching(slabs, subs, along_slab, parity):
    pairs = []
    for s in range(slabs):
        for c in range(subs):
            here, count = (s, slabs) if along_slab else (c, subs)
            there = here + 1 if here % 2 == parity else here - 1
            if 0 <= there < count:
                target = (there, c) if along_slab else (s, there)
            elif along_slab:
                target = (s, c ^ 1) if subs % 2 == 0 else None
            else:
                target = (s, subs - 1 - c) if subs % 2 == 0 else None
            if target is not None:
                pairs.append((s * subs + c, target[0] * subs + target[1]))
    return pairs


def roll(value, shift, axis):
    size = value.shape[axis]
    if isinstance(shift, int):
        return pltpu.roll(value, shift % size, axis)
    return pltpu.roll(value, lax.rem(shift + size, size), axis)


def dot(left, right):
    total = left[0] * right[0]
    for k in range(1, len(left)):
        total = total + left[k] * right[k]
    return total


def axpy4(coefs, values):
    total = coefs[0] * values[0]
    for k in range(1, len(coefs)):
        total = total + coefs[k] * values[k]
    return total


def tile_iota(shape):
    return lax.broadcasted_iota(jnp.int32, shape, 0), lax.broadcasted_iota(jnp.int32, shape, 1)


def parities():
    return lax.rem(lax.axis_index("slab"), 2) == 0, lax.rem(lax.axis_index("sub"), 2) == 0


def pack_kernel(dims, sizes, parts, modes_hbm, span_hbm, chord_hbm, span_geo_hbm, chord_geo_hbm, len_hbm,
                field, live_ref, span_ref, chord_ref, span_geo_ref, chord_geo_ref, row_even, row_odd, col_even, col_odd,
                raw, len_ref, sems):
    modes, dof, rows, cols = dims
    row, lane = tile_iota((rows, cols))
    slab_even, sub_even = parities()
    per = dof * rows
    share = modes // parts
    fetches = [
        pltpu.make_async_copy(modes_hbm.at[pl.ds(i * share * per, share * per), :],
                              raw.at[pl.ds(i * share * per, share * per), :], sems.at[i])
        for i in range(parts)
    ]
    small = ((span_hbm, span_ref), (chord_hbm, chord_ref), (span_geo_hbm, span_geo_ref), (chord_geo_hbm, chord_geo_ref),
             (len_hbm, len_ref))
    others = [pltpu.make_async_copy(src, dst, sems.at[parts + i]) for i, (src, dst) in enumerate(small)]
    for copy in others + fetches:
        copy.start()
    for copy in others:
        copy.wait()

    stations = sizes[0] * rows
    row_start = lax.axis_index("slab") * rows
    col_start = lax.axis_index("sub") * cols

    def length(index):
        value = len_ref[jnp.clip(index, 0, stations - 1)]
        return jnp.where((index >= 0) & (index < stations), value, 0)

    lengths = [length(row_start + r) for r in range(-1, rows + 1)]
    own = jnp.zeros((rows, cols), jnp.int32)
    ahead = jnp.zeros((rows, cols), jnp.int32)
    for r in range(rows):
        own = jnp.where(row == r, lengths[r + 1], own)
        ahead = jnp.where(row == r, lengths[r + 2], ahead)
    column = col_start + lane
    up_live = (column < lengths[0]) & (column < lengths[1])
    left_live = (col_start < own) & (col_start > 0)
    live = ((column < own) & (column < ahead), column + 1 < own, up_live, left_live)
    for i, flags in enumerate(live):
        live_ref[i] = flags.astype(F32)

    packed = [jnp.zeros((rows, cols), F32) for k in range(dof)]
    for m in range(modes):
        if m % share == 0:
            fetches[m // share].wait()
        block = raw[m * per:(m + 1) * per, :].astype(F32)
        field[m * per:(m + 1) * per, :] = block
        mine = (lane >> 1) == m
        for k in range(dof):
            packed[k] = jnp.where(mine, roll(block[k * rows:(k + 1) * rows], 2 * m + 1, 1), packed[k])
        if m % 8 == 7:
            for k in range(dof):
                base = (m - 7) * per + k * rows
                first = field[pl.ds(base, 8, stride=per), :]
                last = field[pl.ds(base + rows - 1, 8, stride=per), :]
                out = k * modes + m - 7
                row_even[out:out + 8, :] = jnp.where(slab_even, last, first)
                row_odd[out:out + 8, :] = jnp.where(slab_even, first, last)
    field[modes * per:modes * per + rows, :] = jnp.zeros((rows, cols), F32)
    coef = jnp.zeros((rows, cols), F32)
    edge = jnp.zeros((rows, cols), F32)
    for k in range(dof + 1):
        span_plane = span_ref[k] if k < dof else span_geo_ref[...]
        chord_plane = chord_ref[k] if k < dof else chord_geo_ref[...]
        coef = jnp.where(row == k, span_plane[rows - 1:rows], coef)
        edge = jnp.where(lane == 2 * k, roll(chord_plane, 2 * k + 1, 1), edge)
    for k in range(dof):
        behind = roll(packed[k], -1, 1)
        col_even[k * rows:(k + 1) * rows, :] = jnp.where(sub_even, packed[k], behind)
        col_odd[k * rows:(k + 1) * rows, :] = jnp.where(sub_even, behind, packed[k])
    row_even[dof * modes:dof * modes + rows, :] = coef
    row_odd[dof * modes:dof * modes + rows, :] = coef
    col_even[dof * rows:(dof + 1) * rows, :] = edge
    col_odd[dof * rows:(dof + 1) * rows, :] = edge


def factor_blocks(blocks):
    count = len(blocks)
    scaled = [[None] * count for i in range(count)]
    factor = [[None] * count for i in range(count)]
    for j in range(count):
        running = blocks[j][j]
        for k in range(j):
            running = running - scaled[j][k] * factor[j][k]
        factor[j][j] = 1.0 / running
        for i in range(j + 1, count):
            running = blocks[i][j]
            for k in range(j):
                running = running - scaled[i][k] * factor[j][k]
            scaled[i][j] = running
            factor[i][j] = running * factor[j][j]
    return factor


def times_ones(value, transposed):
    high = value.astype(jnp.bfloat16)
    rest = value - high.astype(F32)
    middle = rest.astype(jnp.bfloat16)
    low = (rest - middle.astype(F32)).astype(jnp.bfloat16)
    pieces = jnp.concatenate([high, middle, low], axis=1)
    if transposed:
        ones = jnp.ones((8, pieces.shape[1]), jnp.bfloat16)
        return lax.dot_general(ones, pieces, (((1,), (1,)), ((), ())), preferred_element_type=F32)
    ones = jnp.ones((pieces.shape[1], value.shape[1]), jnp.bfloat16)
    return lax.dot_general(pieces, ones, (((1,), (0,)), ((), ())), preferred_element_type=F32)


def factor_place(dof, i, j):
    return 8 * dof + 1 + i * (i + 1) // 2 + j


def solve_blocks(factor, vector):
    count = len(vector)
    forward = []
    for i in range(count):
        running = vector[i]
        for j in range(i):
            running = running - factor(i, j) * forward[j]
        forward.append(running)
    backward = [None] * count
    for i in reversed(range(count)):
        running = forward[i] * factor(i, i)
        for j in range(i + 1, count):
            running = running - factor(j, i) * backward[j]
        backward[i] = running
    return backward


def inner_kernel(dims, modes_ref, live_ref, span_ref, chord_ref, span_geo_ref, chord_geo_ref, load_ref):
    modes, dof, rows, cols = dims
    row, lane = tile_iota((rows, cols))
    per = dof * rows
    first_row, last_row = row == 0, row == rows - 1
    first_col, last_col = lane == 0, lane == cols - 1
    zero = jnp.zeros((rows, cols), F32)
    span_inner = (live_ref[0] > 0.0) & jnp.logical_not(last_row)
    chord_inner = (live_ref[1] > 0.0) & jnp.logical_not(last_col)
    span = [jnp.where(span_inner, span_ref[k], zero) for k in range(dof)]
    chord = [jnp.where(chord_inner, chord_ref[k], zero) for k in range(dof)]
    span_b = [jnp.where(first_row, zero, roll(span[k], 1, 0)) for k in range(dof)]
    chord_b = [jnp.where(first_col, zero, roll(chord[k], 1, 1)) for k in range(dof)]
    span_geo = jnp.where(span_inner, span_geo_ref[...], zero)
    chord_geo = jnp.where(chord_inner, chord_geo_ref[...], zero)
    for m in range(modes):
        start = m * per
        v = [modes_ref[pl.ds(start + k * rows, rows), :] for k in range(dof)]
        jumps = [modes_ref[pl.ds(start + k * rows + 1, rows), :] - v[k] for k in range(dof)]
        span_w = jnp.where(last_row, zero, dot(jumps, jumps) * span_geo)
        jumps = [roll(v[k], -1, 1) - v[k] for k in range(dof)]
        chord_w = jnp.where(last_col, zero, dot(jumps, jumps) * chord_geo)
        span_wb, chord_wb = roll(span_w, 1, 0), roll(chord_w, 1, 1)
        for k in range(dof):
            load_ref[pl.ds(start + k * rows, rows), :] = (
                (span_b[k] * span_wb - span[k] * span_w) + (chord_b[k] * chord_wb - chord[k] * chord_w)
            )


def first_kernel(dims, inner_ref, live_ref, span_ref, chord_ref, span_geo_ref, chord_geo_ref, ground_ref,
                 row_even_out, row_odd_out, col_even_out, col_odd_out,
                 row_even_in, row_odd_in, col_even_in, col_odd_in,
                 load_ref, z_ref, q_ref, coef_ref, row_even, row_odd, col_even, col_odd,
                 up_ref, down_ref, rim_ref, rim2_ref):
    modes, dof, rows, cols = dims
    row, lane = tile_iota((rows, cols))
    slab_even, sub_even = parities()
    per = dof * rows
    span_live, chord_live, up_live, left_live = (live_ref[i] > 0.0 for i in range(4))

    def row_weight(arrived, sent):
        total = None
        for k in range(dof):
            jump = arrived[k * modes:(k + 1) * modes, :] - sent[k * modes:(k + 1) * modes, :]
            total = jump * jump if total is None else total + jump * jump
        return total

    def col_weight(arrived, sent):
        total = None
        for k in range(dof):
            jump = arrived[k * rows:(k + 1) * rows, :] - sent[k * rows:(k + 1) * rows, :]
            total = jump * jump if total is None else total + jump * jump
        return total

    even_weight = row_weight(row_even_in, row_even_out)
    odd_weight = row_weight(row_odd_in, row_odd_out)
    up_weight = jnp.where(slab_even, odd_weight, even_weight)
    down_weight = jnp.where(slab_even, even_weight, odd_weight)
    tail = dof * modes
    up_coef = jnp.where(slab_even, row_odd_in[tail:tail + rows, :], row_even_in[tail:tail + rows, :])
    up_ref[...] = jnp.where(live_ref[2, 0:1, :] > 0.0, up_weight * up_coef[dof:dof + 1], 0.0)
    down_ref[...] = jnp.where(live_ref[0, rows - 1:rows, :] > 0.0, down_weight * span_geo_ref[rows - 1:rows, :], 0.0)
    even_col = col_weight(col_even_in, col_even_out)
    odd_col = col_weight(col_odd_in, col_odd_out)
    left_coef = jnp.where(sub_even, col_odd_in[per:per + rows, :], col_even_in[per:per + rows, :])
    left_weight = jnp.where(sub_even, odd_col, even_col) * left_coef[:, 2 * dof:2 * dof + 1]
    right_weight = jnp.where(sub_even, even_col, odd_col) * chord_geo_ref[:, cols - 1:cols]
    left_weight = jnp.where(left_live, left_weight, 0.0)
    right_weight = jnp.where(live_ref[1, :, cols - 1:cols] > 0.0, right_weight, 0.0)
    lane_even = (lane & 1) == 0
    rim_weight = jnp.where(lane_even, left_weight, roll(right_weight, -1, 1))

    first_row, last_row = row == 0, row == rows - 1
    first_col, last_col = lane == 0, lane == cols - 1

    zero = jnp.zeros((rows, cols), F32)
    span, span_b, chord, chord_b = [], [], [], []
    for k in range(dof):
        span.append(jnp.where(span_live, span_ref[k], zero))
        up = jnp.where(up_live, up_coef[k:k + 1], zero)
        span_b.append(jnp.where(first_row, up, roll(span[k], 1, 0)))
        chord.append(jnp.where(chord_live, chord_ref[k], zero))
        left = jnp.where(left_live, left_coef[:, 2 * k:2 * k + 1], zero)
        chord_b.append(jnp.where(first_col, left, roll(chord[k], 1, 1)))
    blocks = [[None] * dof for i in range(dof)]
    for i in range(dof):
        for j in range(i + 1):
            entry = span[i] * span[j] + span_b[i] * span_b[j] + chord[i] * chord[j] + chord_b[i] * chord_b[j]
            blocks[i][j] = entry + ground_ref[i] if i == j else entry
    factor = factor_blocks(blocks)
    for i in range(dof):
        for j in range(i + 1):
            coef_ref[factor_place(dof, i, j)] = factor[i][j]
    row_rim = [jnp.where(last_row, span[k], jnp.where(first_row, span_b[k], zero)) for k in range(dof)]
    col_rim = [jnp.where(last_col, chord[k], jnp.where(first_col, chord_b[k], zero)) for k in range(dof)]
    row_sign = [jnp.where(last_row, -row_rim[k], row_rim[k]) for k in range(dof)]
    col_sign = [jnp.where(last_col, -col_rim[k], col_rim[k]) for k in range(dof)]
    row_inv = solve_blocks(lambda i, j: factor[i][j], row_rim)
    col_inv = solve_blocks(lambda i, j: factor[i][j], col_rim)
    for group, planes in enumerate((span, span_b, chord, chord_b, row_rim, col_rim, row_inv, col_inv)):
        for k in range(dof):
            coef_ref[group * dof + k] = planes[k]
    row_kappa = dot(row_rim, row_inv)
    col_kappa = dot(col_rim, col_inv)
    coef_ref[8 * dof] = dot(row_rim, col_inv)

    def planes_of(group):
        return [coef_ref[group * dof + k] for k in range(dof)]

    def body(m, carry):
        start = m * per
        row_w = jnp.where(last_row, down_ref[pl.ds(m, 1), :], up_ref[pl.ds(m, 1), :])
        col_w = roll(rim_weight, -2 * m, 1)
        span, span_b, chord, chord_b = (planes_of(i) for i in range(4))
        load = [
            inner_ref[pl.ds(start + k * rows, rows), :] + (row_sign[k] * row_w + col_sign[k] * col_w)
            for k in range(dof)
        ]
        z = solve_blocks(lambda i, j: coef_ref[factor_place(dof, i, j)], load)
        fwd_s, bwd_s, fwd_c, bwd_c = dot(span, z), dot(span_b, z), dot(chord, z), dot(chord_b, z)
        near = [
            jnp.where(last_row, zero, roll(bwd_s, -1, 0)),
            jnp.where(first_row, zero, roll(fwd_s, 1, 0)),
            jnp.where(last_col, zero, roll(bwd_c, -1, 1)),
            jnp.where(first_col, zero, roll(fwd_c, 1, 1)),
        ]
        q = [axpy4([span[k], span_b[k], chord[k], chord_b[k]], near) for k in range(dof)]
        for k in range(dof):
            at = pl.ds(start + k * rows, rows)
            load_ref[at, :] = load[k]
            z_ref[at, :] = z[k]
            q_ref[at, :] = q[k]
        at = pl.ds(m * rows, rows)
        rim_ref[at, :] = jnp.where(last_row, fwd_s, bwd_s)
        rim2_ref[at, :] = dot(planes_of(6), q)
        mine = (lane >> 1) == m
        col_z = roll(jnp.where(last_col, fwd_c, bwd_c), 2 * m + 1, 1)
        col_g = roll(dot(planes_of(7), q), 2 * m + 1, 1)
        return jnp.where(mine, col_z, carry[0]), jnp.where(mine, col_g, carry[1])

    col_z, col_g = zero, zero
    for m in range(modes):
        col_z, col_g = body(m, (col_z, col_g))
    for which, packed in enumerate((col_z, col_g, roll(col_kappa, 1, 1))):
        behind = roll(packed, -1, 1)
        col_even[which * rows:(which + 1) * rows, :] = jnp.where(sub_even, packed, behind)
        col_odd[which * rows:(which + 1) * rows, :] = jnp.where(sub_even, behind, packed)
    for which, ref in enumerate((rim_ref, rim2_ref)):
        for block in range(modes // 8):
            first = ref[pl.ds(block * 8 * rows, 8, stride=rows), :]
            last = ref[pl.ds(block * 8 * rows + rows - 1, 8, stride=rows), :]
            out = which * modes + block * 8
            row_even[out:out + 8, :] = jnp.where(slab_even, last, first)
            row_odd[out:out + 8, :] = jnp.where(slab_even, first, last)
    first = jnp.where(first_row, row_kappa[0:1], zero)
    last = jnp.where(first_row, row_kappa[rows - 1:rows], zero)
    row_even[2 * modes:2 * modes + rows, :] = jnp.where(slab_even, last, first)
    row_odd[2 * modes:2 * modes + rows, :] = jnp.where(slab_even, first, last)


def solve_kernel(dims, load_ref, z_ref, q_ref, coef_ref, g_ref, first_ref, sum_ref):
    modes, dof, rows, cols = dims
    for m in range(modes):
        at = [pl.ds((m * dof + k) * rows, rows) for k in range(dof)]
        q = [q_ref[at[k], :] for k in range(dof)]
        g = solve_blocks(lambda i, j: coef_ref[factor_place(dof, i, j)], q)
        for k in range(dof):
            g_ref[at[k], :] = g[k]
        z, load = [z_ref[at[k], :] for k in range(dof)], [load_ref[at[k], :] for k in range(dof)]
        sum_ref[pl.ds(m * rows, rows), :] = dot(z, load)
    for block in range(modes // 8):
        first_ref[block * 8:block * 8 + 8, :] = sum_of_rows(sum_ref, block * 8 * rows, rows)


def sum_of_rows(ref, base, rows):
    total = ref[pl.ds(base, 8, stride=rows), :]
    for r in range(1, rows):
        total = total + ref[pl.ds(base + r, 8, stride=rows), :]
    return total


def second_kernel(dims, devices, first_ref, z_ref, qp_ref, gp_ref, coef_ref,
                  row_even_out, row_odd_out, col_even_out, col_odd_out,
                  row_even_in, row_odd_in, col_even_in, col_odd_in,
                  q_ref, g_ref, q2_ref, chunk_ref,
                  up_ref, down_ref, up2_ref, down2_ref, sum_ref):
    modes, dof, rows, cols = dims
    row, lane = tile_iota((rows, cols))
    slab_even, sub_even = parities()
    per = dof * rows
    first_row, last_row = row == 0, row == rows - 1
    first_col, last_col = lane == 0, lane == cols - 1
    lane_even = (lane & 1) == 0
    zero = jnp.zeros((rows, cols), F32)

    def pick(flag, even, odd, start, size):
        return jnp.where(flag, even[start:start + size, :], odd[start:start + size, :])

    up_flag = jnp.logical_not(slab_even)
    left_flag = jnp.logical_not(sub_even)
    up_ref[...] = pick(up_flag, row_even_in, row_odd_in, 0, modes)
    down_ref[...] = pick(slab_even, row_even_in, row_odd_in, 0, modes)
    up2_ref[...] = (
        pick(up_flag, row_even_in, row_odd_in, modes, modes)
        + pick(up_flag, row_even_in, row_odd_in, 2 * modes, 1) * pick(up_flag, row_even_out, row_odd_out, 0, modes)
    )
    down2_ref[...] = (
        pick(slab_even, row_even_in, row_odd_in, modes, modes)
        + pick(slab_even, row_even_in, row_odd_in, 2 * modes, 1) * pick(slab_even, row_even_out, row_odd_out, 0, modes)
    )

    def merge(left, right):
        return jnp.where(lane_even, left, roll(right, -1, 1))

    def second_col(flag):
        kappa = pick(flag, col_even_in, col_odd_in, 2 * rows, rows)[:, 0:1]
        return pick(flag, col_even_in, col_odd_in, rows, rows) + kappa * pick(flag, col_even_out, col_odd_out, 0, rows)

    rim = merge(pick(left_flag, col_even_in, col_odd_in, 0, rows), pick(sub_even, col_even_in, col_odd_in, 0, rows))
    rim2 = merge(second_col(left_flag), second_col(sub_even))
    corner_kappa = coef_ref[8 * dof]

    def planes_of(group):
        return [coef_ref[group * dof + k] for k in range(dof)]

    def body(m, carry):
        start = m * per
        at = [pl.ds(start + k * rows, rows) for k in range(dof)]
        row_ghost = jnp.where(last_row, down_ref[pl.ds(m, 1), :], up_ref[pl.ds(m, 1), :])
        col_ghost = roll(rim, -2 * m, 1)
        col_ghost2 = roll(rim2, -2 * m, 1)
        row_rim, col_rim, row_inv, col_inv = (planes_of(i) for i in range(4, 8))
        q = [qp_ref[at[k], :] + (row_rim[k] * row_ghost + col_rim[k] * col_ghost) for k in range(dof)]
        g = [gp_ref[at[k], :] + (row_inv[k] * row_ghost + col_inv[k] * col_ghost) for k in range(dof)]
        span, span_b, chord, chord_b = (planes_of(i) for i in range(4))
        fwd_s, bwd_s, fwd_c, bwd_c = dot(span, g), dot(span_b, g), dot(chord, g), dot(chord_b, g)
        near = [
            jnp.where(last_row, down2_ref[pl.ds(m, 1), :], roll(bwd_s, -1, 0)),
            jnp.where(first_row, up2_ref[pl.ds(m, 1), :], roll(fwd_s, 1, 0)),
            jnp.where(last_col, col_ghost2, roll(bwd_c, -1, 1)),
            jnp.where(first_col, col_ghost2, roll(fwd_c, 1, 1)),
        ]
        q2 = [axpy4([span[k], span_b[k], chord[k], chord_b[k]], near) for k in range(dof)]
        z = [z_ref[at[k], :] for k in range(dof)]
        miss = (corner_kappa * col_ghost, corner_kappa * row_ghost)
        cross = miss[0] * jnp.where(last_row, near[0], near[1]) + miss[1] * jnp.where(last_col, near[2], near[3])
        for which, (left, right) in enumerate(((z, q), (g, q), (g, q2))):
            spot = (which * modes + m) * rows
            total = dot(left, right)
            sum_ref[pl.ds(spot, rows), :] = total + cross if which == 2 else total
        for k in range(dof):
            q_ref[at[k], :] = q[k]
            g_ref[at[k], :] = g[k]
            q2_ref[at[k], :] = q2[k]
        mine = (lane >> 1) == m
        return tuple(jnp.where(mine, roll(new, 2 * m + 1, 1), old) for new, old in zip(miss, carry))

    corners = (zero, zero)
    for m in range(modes):
        corners = body(m, corners)
    sums = [first_ref[...]] + [sum_of_rows(sum_ref, block * 8 * rows, rows) for block in range(3 * modes // 8)]
    sums = jnp.concatenate(sums, axis=0)
    sums = jnp.sum(jnp.transpose(sums), axis=0, keepdims=True)
    chunk = jnp.where(row % LINES == 0, sums[0:1], zero)
    for which, corner in enumerate(corners):
        far = roll(jnp.broadcast_to(corner[rows - 1:rows], (rows, cols)), cols // 2, 1)
        line = jnp.where(lane < cols // 2, corner[0:1], far)
        chunk = jnp.where(row % LINES == which + 1, line, chunk)

    def send(d, carry):
        chunk_ref[pl.ds(pl.multiple_of(d * rows, rows), rows), :] = chunk
        return carry

    lax.fori_loop(0, devices * LINES // rows, send, 0, unroll=8)


def last_kernel(dims, sizes, steps, part_ref, coef_ref, load_ref, z_ref, q_ref, g_ref, q2_ref,
                adjoint_hbm, residual_hbm, a_ref, b_ref, load_share_ref, q_share_ref, shares_ref, adjoint_ref, residual_ref, sems):
    modes, dof, rows, cols = dims
    slabs, subs = sizes
    devices = slabs * subs
    row, lane = tile_iota((rows, cols))
    per = dof * rows
    half = cols // 2

    shares_ref[0:devices * LINES, :] = part_ref[...]

    def lines(which):
        return shares_ref[pl.ds(which, devices, stride=LINES), :]

    miss_row, miss_col = lines(1), lines(2)
    wide = lax.broadcasted_iota(jnp.int32, (devices, cols), 1)
    swapped = roll(miss_row, half, 1)
    met_row = jnp.where(wide >= half, roll(swapped, -subs, 0), roll(swapped, subs, 0))
    met_col = jnp.where((wide & 1) == 0, roll(roll(miss_col, -1, 1), -1, 0), roll(roll(miss_col, 1, 1), 1, 0))
    total = jnp.sum(lines(0), axis=0, keepdims=True)
    missed = jnp.sum(miss_row * met_row + miss_col * met_col, axis=0, keepdims=True)
    big_row, big_lane = tile_iota((4 * modes, cols))
    spread = jnp.where(big_row == big_lane, total, 0.0)
    spread = spread + jnp.where(((big_lane & (half - 1)) >> 1) == big_row - 3 * modes, missed, 0.0)
    spread = times_ones(spread, False)
    m0, m1, m2, m3 = (spread[i * modes:(i + 1) * modes] for i in range(4))
    m1, m2, m3 = m1 / m0, m2 / m0, m3 / m0
    step0 = 1.0 / (1.0 - m1)
    square = step0 * step0
    beta = (m2 - m1 * m1) * square
    c0 = (m2 - m1) * square
    excess = beta * beta - (c0 * c0 * m1 + 2.0 * c0 * step0 * m2 + square * m3)
    inverse = 1.0 / (beta + excess)
    step1 = beta * inverse
    a_ref[...] = step0 + step1 * c0
    b_ref[...] = step1 * step0
    load_share_ref[...] = -m1 * step0 - step1 * c0
    q_share_ref[...] = step0 * (excess * inverse) + step1 * c0

    here = lax.axis_index("slab") * subs + lax.axis_index("sub")

    def line_of(device, which):
        device = lax.rem(device + devices, devices)
        return jnp.broadcast_to(part_ref[pl.ds(device * LINES + which, 1), :], (rows, cols))

    row_fixes = jnp.where(row == rows - 1, line_of(here + subs, 1), roll(line_of(here - subs, 1), half, 1))
    col_fixes = jnp.where((lane & 1) == 0, roll(line_of(here + 1, 2), -1, 1), roll(line_of(here - 1, 2), 1, 1))
    col_fixes = jnp.where(row == rows - 1, roll(col_fixes, half, 1), col_fixes)
    corner = ((row == 0) | (row == rows - 1)) & ((lane == 0) | (lane == cols - 1))
    count = modes // steps
    copies = []
    for m in range(modes):
        a = a_ref[m:m + 1, :]
        b = b_ref[m:m + 1, :]
        load_share = load_share_ref[m:m + 1, :]
        q_share = q_share_ref[m:m + 1, :]
        row_fix = b * jnp.where(corner, roll(row_fixes, -1 - 2 * m, 1), 0.0)
        col_fix = b * jnp.where(corner, roll(col_fixes, -1 - 2 * m, 1), 0.0)
        for k in range(dof):
            at = pl.ds(m * per + k * rows, rows)
            adjoint_ref[at, :] = a * z_ref[at, :] + b * g_ref[at, :]
            residual_ref[at, :] = (
                (load_share * load_ref[at, :] + q_share * q_ref[at, :])
                + (b * q2_ref[at, :] + (coef_ref[4 * dof + k] * row_fix + coef_ref[5 * dof + k] * col_fix))
            )
        if (m + 1) % count == 0:
            at = pl.ds((m + 1 - count) * per, count * per)
            for src, dst in ((adjoint_ref, adjoint_hbm), (residual_ref, residual_hbm)):
                copy = pltpu.make_async_copy(src.at[at, :], dst.at[at, :], sems.at[len(copies)])
                copy.start()
                copies.append(copy)
    for copy in copies:
        copy.wait()


def body_of(sizes):
    slabs, subs = sizes
    devices = slabs * subs
    axes = ("slab", "sub")
    paths = [matching(slabs, subs, along, parity) for along in (True, False) for parity in (0, 1)]

    def exchange(arrays):
        return [lax.ppermute(array, axes, path) for array, path in zip(arrays, paths)]

    vmem = pl.BlockSpec(memory_space=pltpu.VMEM)
    hbm = pl.BlockSpec(memory_space=pltpu.HBM)

    def body(mode_shapes, span_stiff, chord_stiff, span_geo, chord_geo, ground, chord_len):
        modes, dof, rows, cols = mode_shapes.shape
        dims = mode_shapes.shape
        count = modes * dof * rows

        def call(kernel, name, inputs, in_specs, outs, scratch, out_spec=vmem):
            return pl.pallas_call(
                kernel,
                out_shape=[jax.ShapeDtypeStruct(shape, F32) for shape in outs],
                in_specs=in_specs,
                out_specs=[out_spec] * len(outs),
                scratch_shapes=[pltpu.VMEM(s, F32) if isinstance(s, tuple) else s for s in scratch],
                compiler_params=pltpu.CompilerParams(vmem_limit_bytes=VMEM_LIMIT),
                name=name,
            )(*inputs)

        plane, planes, full = (rows, cols), (dof, rows, cols), (count, cols)
        row_shape, col_shape = (modes * dof + rows, cols), ((dof + 1) * rows, cols)
        parts = 2
        inputs = (mode_shapes.reshape(count, cols), span_stiff, chord_stiff, span_geo, chord_geo, chord_len)
        field, *coefs, row_even, row_odd, col_even, col_odd = call(
            lambda *refs: pack_kernel(dims, sizes, parts, *refs), "pack_rim",
            [pltpu.with_memory_space_constraint(x, pltpu.HBM) for x in inputs], [hbm] * 6,
            [(count + 8 * dof * rows, cols), (4, rows, cols), planes, planes, plane, plane, row_shape, row_shape, col_shape, col_shape],
            [pltpu.VMEM(full, mode_shapes.dtype), pltpu.SMEM(chord_len.shape, jnp.int32), pltpu.SemaphoreType.DMA((parts + 5,))],
        )
        rims = [row_even, row_odd, col_even, col_odd]
        met = exchange(rims)
        (inner,) = call(
            lambda *refs: inner_kernel(dims, *refs), "inner_load", (field, *coefs), [vmem] * 6, [full], [],
        )
        row_shape, col_shape = (2 * modes + rows, cols), (3 * rows, cols)
        load, z, qp, coef, *rims2 = call(
            lambda *refs: first_kernel(dims, *refs), "load_and_first",
            (inner, *coefs, ground, *rims, *met), [vmem] * 15,
            [full] * 3 + [(factor_place(dof, dof, 0), rows, cols), row_shape, row_shape, col_shape, col_shape],
            [(modes, cols), (modes, cols), ((modes + 1) * rows, cols), ((modes + 1) * rows, cols)],
        )
        met2 = exchange(rims2)
        gp, first = call(
            lambda *refs: solve_kernel(dims, *refs), "solve_inner", (load, z, qp, coef), [vmem] * 4,
            [full, (modes, cols)], [((modes + 1) * rows, cols)],
        )
        q, g, q2, chunk = call(
            lambda *refs: second_kernel(dims, devices, *refs), "second_and_sums",
            (first, z, qp, gp, coef, *rims2, *met2), [vmem] * 13,
            [full] * 3 + [(devices * LINES, cols)],
            [(modes, cols)] * 4 + [((3 * modes + 1) * rows, cols)],
        )
        shares = lax.all_to_all(chunk.reshape(devices, LINES, cols), axes, 0, 0).reshape(devices * LINES, cols)
        steps = 4
        adjoint, residual = call(
            lambda *refs: last_kernel(dims, sizes, steps, *refs), "combine",
            (shares, coef, load, z, q, g, q2), [vmem] * 7, [full] * 2,
            [(modes, cols)] * 4 + [(devices * LINES + 8, cols), full, full, pltpu.SemaphoreType.DMA((2 * steps,))], hbm,
        )
        return adjoint.reshape(dims), residual.reshape(dims)

    return body


def solution(mesh):
    return jax.shard_map(
        body_of((mesh.shape["slab"], mesh.shape["sub"])),
        mesh=mesh,
        in_specs=(
            P(None, None, "slab", "sub"),
            P(None, "slab", "sub"),
            P(None, "slab", "sub"),
            P("slab", "sub"),
            P("slab", "sub"),
            P(None, "slab", "sub"),
            P(),
        ),
        out_specs=(P(None, None, "slab", "sub"), P(None, None, "slab", "sub")),
        check_vma=False,
    )
```

```python
import jax
import jax.numpy as jnp
from jax import lax
from jax.experimental import pallas as pl
from jax.experimental.pallas import tpu as pltpu
from jax.sharding import PartitionSpec as P

F32 = jnp.float32
VMEM_LIMIT = 24 * 1024 * 1024
LINES = 4


def matching(slabs, subs, along_slab, parity):
    pairs = []
    for s in range(slabs):
        for c in range(subs):
            here, count = (s, slabs) if along_slab else (c, subs)
            there = here + 1 if here % 2 == parity else here - 1
            if 0 <= there < count:
                target = (there, c) if along_slab else (s, there)
            elif along_slab:
                target = (s, c ^ 1) if subs % 2 == 0 else None
            else:
                target = (s, subs - 1 - c) if subs % 2 == 0 else None
            if target is not None:
                pairs.append((s * subs + c, target[0] * subs + target[1]))
    return pairs


def roll(value, shift, axis):
    size = value.shape[axis]
    if isinstance(shift, int):
        return pltpu.roll(value, shift % size, axis)
    return pltpu.roll(value, lax.rem(shift + size, size), axis)


def dot(left, right):
    total = left[0] * right[0]
    for k in range(1, len(left)):
        total = total + left[k] * right[k]
    return total


def axpy4(coefs, values):
    total = coefs[0] * values[0]
    for k in range(1, len(coefs)):
        total = total + coefs[k] * values[k]
    return total


def tile_iota(shape):
    return lax.broadcasted_iota(jnp.int32, shape, 0), lax.broadcasted_iota(jnp.int32, shape, 1)


def parities():
    return lax.rem(lax.axis_index("slab"), 2) == 0, lax.rem(lax.axis_index("sub"), 2) == 0


def pack_kernel(dims, sizes, parts, modes_hbm, span_hbm, chord_hbm, span_geo_hbm, chord_geo_hbm, len_hbm,
                field, live_ref, span_ref, chord_ref, span_geo_ref, chord_geo_ref, row_even, row_odd, col_even, col_odd,
                raw, len_ref, sems):
    modes, dof, rows, cols = dims
    row, lane = tile_iota((rows, cols))
    slab_even, sub_even = parities()
    per = dof * rows
    share = modes // parts
    fetches = [
        pltpu.make_async_copy(modes_hbm.at[pl.ds(i * share * per, share * per), :],
                              raw.at[pl.ds(i * share * per, share * per), :], sems.at[i])
        for i in range(parts)
    ]
    small = ((span_hbm, span_ref), (chord_hbm, chord_ref), (span_geo_hbm, span_geo_ref), (chord_geo_hbm, chord_geo_ref),
             (len_hbm, len_ref))
    others = [pltpu.make_async_copy(src, dst, sems.at[parts + i]) for i, (src, dst) in enumerate(small)]
    for copy in others + fetches:
        copy.start()
    for copy in others:
        copy.wait()

    stations = sizes[0] * rows
    row_start = lax.axis_index("slab") * rows
    col_start = lax.axis_index("sub") * cols

    def length(index):
        value = len_ref[jnp.clip(index, 0, stations - 1)]
        return jnp.where((index >= 0) & (index < stations), value, 0)

    lengths = [length(row_start + r) for r in range(-1, rows + 1)]
    own = jnp.zeros((rows, cols), jnp.int32)
    ahead = jnp.zeros((rows, cols), jnp.int32)
    for r in range(rows):
        own = jnp.where(row == r, lengths[r + 1], own)
        ahead = jnp.where(row == r, lengths[r + 2], ahead)
    column = col_start + lane
    up_live = (column < lengths[0]) & (column < lengths[1])
    left_live = (col_start < own) & (col_start > 0)
    live = ((column < own) & (column < ahead), column + 1 < own, up_live, left_live)
    for i, flags in enumerate(live):
        live_ref[i] = flags.astype(F32)

    packed = [jnp.zeros((rows, cols), F32) for k in range(dof)]
    for m in range(modes):
        if m % share == 0:
            fetches[m // share].wait()
        block = raw[m * per:(m + 1) * per, :].astype(F32)
        field[m * per:(m + 1) * per, :] = block
        mine = (lane >> 1) == m
        for k in range(dof):
            packed[k] = jnp.where(mine, roll(block[k * rows:(k + 1) * rows], 2 * m + 1, 1), packed[k])
        if m % 8 == 7:
            for k in range(dof):
                base = (m - 7) * per + k * rows
                first = field[pl.ds(base, 8, stride=per), :]
                last = field[pl.ds(base + rows - 1, 8, stride=per), :]
                out = k * modes + m - 7
                row_even[out:out + 8, :] = jnp.where(slab_even, last, first)
                row_odd[out:out + 8, :] = jnp.where(slab_even, first, last)
    field[modes * per:modes * per + rows, :] = jnp.zeros((rows, cols), F32)
    coef = jnp.zeros((rows, cols), F32)
    edge = jnp.zeros((rows, cols), F32)
    for k in range(dof + 1):
        span_plane = span_ref[k] if k < dof else span_geo_ref[...]
        chord_plane = chord_ref[k] if k < dof else chord_geo_ref[...]
        coef = jnp.where(row == k, span_plane[rows - 1:rows], coef)
        edge = jnp.where(lane == 2 * k, roll(chord_plane, 2 * k + 1, 1), edge)
    for k in range(dof):
        behind = roll(packed[k], -1, 1)
        col_even[k * rows:(k + 1) * rows, :] = jnp.where(sub_even, packed[k], behind)
        col_odd[k * rows:(k + 1) * rows, :] = jnp.where(sub_even, behind, packed[k])
    row_even[dof * modes:dof * modes + rows, :] = coef
    row_odd[dof * modes:dof * modes + rows, :] = coef
    col_even[dof * rows:(dof + 1) * rows, :] = edge
    col_odd[dof * rows:(dof + 1) * rows, :] = edge


def factor_blocks(blocks):
    count = len(blocks)
    scaled = [[None] * count for i in range(count)]
    factor = [[None] * count for i in range(count)]
    for j in range(count):
        running = blocks[j][j]
        for k in range(j):
            running = running - scaled[j][k] * factor[j][k]
        factor[j][j] = 1.0 / running
        for i in range(j + 1, count):
            running = blocks[i][j]
            for k in range(j):
                running = running - scaled[i][k] * factor[j][k]
            scaled[i][j] = running
            factor[i][j] = running * factor[j][j]
    return factor


def times_ones(value, transposed):
    high = value.astype(jnp.bfloat16)
    rest = value - high.astype(F32)
    middle = rest.astype(jnp.bfloat16)
    low = (rest - middle.astype(F32)).astype(jnp.bfloat16)
    pieces = jnp.concatenate([high, middle, low], axis=1)
    if transposed:
        ones = jnp.ones((8, pieces.shape[1]), jnp.bfloat16)
        return lax.dot_general(ones, pieces, (((1,), (1,)), ((), ())), preferred_element_type=F32)
    ones = jnp.ones((pieces.shape[1], value.shape[1]), jnp.bfloat16)
    return lax.dot_general(pieces, ones, (((1,), (0,)), ((), ())), preferred_element_type=F32)


def factor_place(dof, i, j):
    return 8 * dof + 3 + i * (i + 1) // 2 + j


def solve_blocks(factor, vector):
    count = len(vector)
    forward = []
    for i in range(count):
        running = vector[i]
        for j in range(i):
            running = running - factor(i, j) * forward[j]
        forward.append(running)
    backward = [None] * count
    for i in reversed(range(count)):
        running = forward[i] * factor(i, i)
        for j in range(i + 1, count):
            running = running - factor(j, i) * backward[j]
        backward[i] = running
    return backward


def inner_kernel(dims, modes_ref, live_ref, span_ref, chord_ref, span_geo_ref, chord_geo_ref, load_ref):
    modes, dof, rows, cols = dims
    row, lane = tile_iota((rows, cols))
    per = dof * rows
    first_row, last_row = row == 0, row == rows - 1
    first_col, last_col = lane == 0, lane == cols - 1
    zero = jnp.zeros((rows, cols), F32)
    span_inner = (live_ref[0] > 0.0) & jnp.logical_not(last_row)
    chord_inner = (live_ref[1] > 0.0) & jnp.logical_not(last_col)
    span = [jnp.where(span_inner, span_ref[k], zero) for k in range(dof)]
    chord = [jnp.where(chord_inner, chord_ref[k], zero) for k in range(dof)]
    span_b = [jnp.where(first_row, zero, roll(span[k], 1, 0)) for k in range(dof)]
    chord_b = [jnp.where(first_col, zero, roll(chord[k], 1, 1)) for k in range(dof)]
    span_geo = jnp.where(span_inner, span_geo_ref[...], zero)
    chord_geo = jnp.where(chord_inner, chord_geo_ref[...], zero)
    for m in range(modes):
        start = m * per
        v = [modes_ref[pl.ds(start + k * rows, rows), :] for k in range(dof)]
        jumps = [modes_ref[pl.ds(start + k * rows + 1, rows), :] - v[k] for k in range(dof)]
        span_w = jnp.where(last_row, zero, dot(jumps, jumps) * span_geo)
        jumps = [roll(v[k], -1, 1) - v[k] for k in range(dof)]
        chord_w = jnp.where(last_col, zero, dot(jumps, jumps) * chord_geo)
        span_wb, chord_wb = roll(span_w, 1, 0), roll(chord_w, 1, 1)
        for k in range(dof):
            load_ref[pl.ds(start + k * rows, rows), :] = (
                (span_b[k] * span_wb - span[k] * span_w) + (chord_b[k] * chord_wb - chord[k] * chord_w)
            )


def first_kernel(dims, inner_ref, live_ref, span_ref, chord_ref, span_geo_ref, chord_geo_ref, ground_ref,
                 row_even_out, row_odd_out, col_even_out, col_odd_out,
                 row_even_in, row_odd_in, col_even_in, col_odd_in,
                 load_ref, z_ref, q_ref, coef_ref, row_even, row_odd, col_even, col_odd,
                 up_ref, down_ref, rim_ref, rim2_ref):
    modes, dof, rows, cols = dims
    row, lane = tile_iota((rows, cols))
    slab_even, sub_even = parities()
    per = dof * rows
    span_live, chord_live, up_live, left_live = (live_ref[i] > 0.0 for i in range(4))

    def row_weight(arrived, sent):
        total = None
        for k in range(dof):
            jump = arrived[k * modes:(k + 1) * modes, :] - sent[k * modes:(k + 1) * modes, :]
            total = jump * jump if total is None else total + jump * jump
        return total

    def col_weight(arrived, sent):
        total = None
        for k in range(dof):
            jump = arrived[k * rows:(k + 1) * rows, :] - sent[k * rows:(k + 1) * rows, :]
            total = jump * jump if total is None else total + jump * jump
        return total

    even_weight = row_weight(row_even_in, row_even_out)
    odd_weight = row_weight(row_odd_in, row_odd_out)
    up_weight = jnp.where(slab_even, odd_weight, even_weight)
    down_weight = jnp.where(slab_even, even_weight, odd_weight)
    tail = dof * modes
    up_coef = jnp.where(slab_even, row_odd_in[tail:tail + rows, :], row_even_in[tail:tail + rows, :])
    up_ref[...] = jnp.where(live_ref[2, 0:1, :] > 0.0, up_weight * up_coef[dof:dof + 1], 0.0)
    down_ref[...] = jnp.where(live_ref[0, rows - 1:rows, :] > 0.0, down_weight * span_geo_ref[rows - 1:rows, :], 0.0)
    even_col = col_weight(col_even_in, col_even_out)
    odd_col = col_weight(col_odd_in, col_odd_out)
    left_coef = jnp.where(sub_even, col_odd_in[per:per + rows, :], col_even_in[per:per + rows, :])
    left_weight = jnp.where(sub_even, odd_col, even_col) * left_coef[:, 2 * dof:2 * dof + 1]
    right_weight = jnp.where(sub_even, even_col, odd_col) * chord_geo_ref[:, cols - 1:cols]
    left_weight = jnp.where(left_live, left_weight, 0.0)
    right_weight = jnp.where(live_ref[1, :, cols - 1:cols] > 0.0, right_weight, 0.0)
    lane_even = (lane & 1) == 0
    rim_weight = jnp.where(lane_even, left_weight, roll(right_weight, -1, 1))

    first_row, last_row = row == 0, row == rows - 1
    first_col, last_col = lane == 0, lane == cols - 1

    zero = jnp.zeros((rows, cols), F32)
    span, span_b, chord, chord_b = [], [], [], []
    for k in range(dof):
        span.append(jnp.where(span_live, span_ref[k], zero))
        up = jnp.where(up_live, up_coef[k:k + 1], zero)
        span_b.append(jnp.where(first_row, up, roll(span[k], 1, 0)))
        chord.append(jnp.where(chord_live, chord_ref[k], zero))
        left = jnp.where(left_live, left_coef[:, 2 * k:2 * k + 1], zero)
        chord_b.append(jnp.where(first_col, left, roll(chord[k], 1, 1)))
    blocks = [[None] * dof for i in range(dof)]
    for i in range(dof):
        for j in range(i + 1):
            entry = span[i] * span[j] + span_b[i] * span_b[j] + chord[i] * chord[j] + chord_b[i] * chord_b[j]
            blocks[i][j] = entry + ground_ref[i] if i == j else entry
    factor = factor_blocks(blocks)
    for i in range(dof):
        for j in range(i + 1):
            coef_ref[factor_place(dof, i, j)] = factor[i][j]
    row_rim = [jnp.where(last_row, span[k], jnp.where(first_row, span_b[k], zero)) for k in range(dof)]
    col_rim = [jnp.where(last_col, chord[k], jnp.where(first_col, chord_b[k], zero)) for k in range(dof)]
    row_sign = [jnp.where(last_row, -row_rim[k], row_rim[k]) for k in range(dof)]
    col_sign = [jnp.where(last_col, -col_rim[k], col_rim[k]) for k in range(dof)]
    row_inv = solve_blocks(lambda i, j: factor[i][j], row_rim)
    col_inv = solve_blocks(lambda i, j: factor[i][j], col_rim)
    for group, planes in enumerate((span, span_b, chord, chord_b, row_rim, col_rim, row_inv, col_inv)):
        for k in range(dof):
            coef_ref[group * dof + k] = planes[k]
    row_kappa = dot(row_rim, row_inv)
    col_kappa = dot(col_rim, col_inv)
    coef_ref[8 * dof] = dot(row_rim, col_inv)
    coef_ref[8 * dof + 1] = row_kappa
    coef_ref[8 * dof + 2] = col_kappa

    def planes_of(group):
        return [coef_ref[group * dof + k] for k in range(dof)]

    def body(m, carry):
        start = m * per
        row_w = jnp.where(last_row, down_ref[pl.ds(m, 1), :], up_ref[pl.ds(m, 1), :])
        col_w = roll(rim_weight, -2 * m, 1)
        span, span_b, chord, chord_b = (planes_of(i) for i in range(4))
        load = [
            inner_ref[pl.ds(start + k * rows, rows), :] + (row_sign[k] * row_w + col_sign[k] * col_w)
            for k in range(dof)
        ]
        z = solve_blocks(lambda i, j: coef_ref[factor_place(dof, i, j)], load)
        fwd_s, bwd_s, fwd_c, bwd_c = dot(span, z), dot(span_b, z), dot(chord, z), dot(chord_b, z)
        near = [
            jnp.where(last_row, zero, roll(bwd_s, -1, 0)),
            jnp.where(first_row, zero, roll(fwd_s, 1, 0)),
            jnp.where(last_col, zero, roll(bwd_c, -1, 1)),
            jnp.where(first_col, zero, roll(fwd_c, 1, 1)),
        ]
        q = [axpy4([span[k], span_b[k], chord[k], chord_b[k]], near) for k in range(dof)]
        for k in range(dof):
            at = pl.ds(start + k * rows, rows)
            load_ref[at, :] = load[k]
            z_ref[at, :] = z[k]
            q_ref[at, :] = q[k]
        at = pl.ds(m * rows, rows)
        rim_ref[at, :] = jnp.where(last_row, fwd_s, bwd_s)
        rim2_ref[at, :] = dot(planes_of(6), q)
        mine = (lane >> 1) == m
        col_z = roll(jnp.where(last_col, fwd_c, bwd_c), 2 * m + 1, 1)
        col_g = roll(dot(planes_of(7), q), 2 * m + 1, 1)
        return jnp.where(mine, col_z, carry[0]), jnp.where(mine, col_g, carry[1])

    col_z, col_g = zero, zero
    for m in range(modes):
        col_z, col_g = body(m, (col_z, col_g))
    for which, packed in enumerate((col_z, col_g, roll(col_kappa, 1, 1))):
        behind = roll(packed, -1, 1)
        col_even[which * rows:(which + 1) * rows, :] = jnp.where(sub_even, packed, behind)
        col_odd[which * rows:(which + 1) * rows, :] = jnp.where(sub_even, behind, packed)
    for which, ref in enumerate((rim_ref, rim2_ref)):
        for block in range(modes // 8):
            first = ref[pl.ds(block * 8 * rows, 8, stride=rows), :]
            last = ref[pl.ds(block * 8 * rows + rows - 1, 8, stride=rows), :]
            out = which * modes + block * 8
            row_even[out:out + 8, :] = jnp.where(slab_even, last, first)
            row_odd[out:out + 8, :] = jnp.where(slab_even, first, last)
    first = jnp.where(first_row, row_kappa[0:1], zero)
    last = jnp.where(first_row, row_kappa[rows - 1:rows], zero)
    row_even[2 * modes:2 * modes + rows, :] = jnp.where(slab_even, last, first)
    row_odd[2 * modes:2 * modes + rows, :] = jnp.where(slab_even, first, last)


def solve_kernel(dims, load_ref, z_ref, q_ref, coef_ref, g_ref, first_ref, cross_ref, sum_ref):
    modes, dof, rows, cols = dims
    for m in range(modes):
        at = [pl.ds((m * dof + k) * rows, rows) for k in range(dof)]
        q = [q_ref[at[k], :] for k in range(dof)]
        g = solve_blocks(lambda i, j: coef_ref[factor_place(dof, i, j)], q)
        for k in range(dof):
            g_ref[at[k], :] = g[k]
        z, load = [z_ref[at[k], :] for k in range(dof)], [load_ref[at[k], :] for k in range(dof)]
        for which, (left, right) in enumerate(((z, load), (z, q), (g, q))):
            sum_ref[pl.ds((which * modes + m) * rows, rows), :] = dot(left, right)
        for which, (group, field) in enumerate(((4, z), (5, z), (6, q), (7, q))):
            planes = [coef_ref[group * dof + k] for k in range(dof)]
            cross_ref[pl.ds((which * modes + m) * rows, rows), :] = dot(planes, field)
    for block in range(3 * modes // 8):
        first_ref[block * 8:block * 8 + 8, :] = sum_of_rows(sum_ref, block * 8 * rows, rows)


def sum_of_rows(ref, base, rows):
    total = ref[pl.ds(base, 8, stride=rows), :]
    for r in range(1, rows):
        total = total + ref[pl.ds(base + r, 8, stride=rows), :]
    return total


def second_kernel(dims, devices, first_ref, cross_ref, gp_ref, coef_ref,
                  row_even_out, row_odd_out, col_even_out, col_odd_out,
                  row_even_in, row_odd_in, col_even_in, col_odd_in,
                  g_ref, q2_ref, chunk_ref, up_ref, down_ref, rim_ref,
                  up2_ref, down2_ref, sum_ref):
    modes, dof, rows, cols = dims
    row, lane = tile_iota((rows, cols))
    slab_even, sub_even = parities()
    per = dof * rows
    first_row, last_row = row == 0, row == rows - 1
    first_col, last_col = lane == 0, lane == cols - 1
    lane_even = (lane & 1) == 0
    zero = jnp.zeros((rows, cols), F32)

    def pick(flag, even, odd, start, size):
        return jnp.where(flag, even[start:start + size, :], odd[start:start + size, :])

    up_flag = jnp.logical_not(slab_even)
    left_flag = jnp.logical_not(sub_even)
    up_ref[...] = pick(up_flag, row_even_in, row_odd_in, 0, modes)
    down_ref[...] = pick(slab_even, row_even_in, row_odd_in, 0, modes)
    up2_ref[...] = (
        pick(up_flag, row_even_in, row_odd_in, modes, modes)
        + pick(up_flag, row_even_in, row_odd_in, 2 * modes, 1) * pick(up_flag, row_even_out, row_odd_out, 0, modes)
    )
    down2_ref[...] = (
        pick(slab_even, row_even_in, row_odd_in, modes, modes)
        + pick(slab_even, row_even_in, row_odd_in, 2 * modes, 1) * pick(slab_even, row_even_out, row_odd_out, 0, modes)
    )

    def merge(left, right):
        return jnp.where(lane_even, left, roll(right, -1, 1))

    def second_col(flag):
        kappa = pick(flag, col_even_in, col_odd_in, 2 * rows, rows)[:, 0:1]
        return pick(flag, col_even_in, col_odd_in, rows, rows) + kappa * pick(flag, col_even_out, col_odd_out, 0, rows)

    rim = merge(pick(left_flag, col_even_in, col_odd_in, 0, rows), pick(sub_even, col_even_in, col_odd_in, 0, rows))
    rim2 = merge(second_col(left_flag), second_col(sub_even))
    corner_kappa, row_kappa, col_kappa = (coef_ref[8 * dof + i] for i in range(3))
    rim_ref[...] = rim

    def planes_of(group):
        return [coef_ref[group * dof + k] for k in range(dof)]

    def body(m, carry):
        start = m * per
        at = [pl.ds(start + k * rows, rows) for k in range(dof)]
        row_ghost = jnp.where(last_row, down_ref[pl.ds(m, 1), :], up_ref[pl.ds(m, 1), :])
        col_ghost = roll(rim, -2 * m, 1)
        col_ghost2 = roll(rim2, -2 * m, 1)
        row_inv, col_inv = planes_of(6), planes_of(7)
        g = [gp_ref[at[k], :] + (row_inv[k] * row_ghost + col_inv[k] * col_ghost) for k in range(dof)]
        span, span_b, chord, chord_b = (planes_of(i) for i in range(4))
        fwd_s, bwd_s, fwd_c, bwd_c = dot(span, g), dot(span_b, g), dot(chord, g), dot(chord_b, g)
        near = [
            jnp.where(last_row, down2_ref[pl.ds(m, 1), :], roll(bwd_s, -1, 0)),
            jnp.where(first_row, up2_ref[pl.ds(m, 1), :], roll(fwd_s, 1, 0)),
            jnp.where(last_col, col_ghost2, roll(bwd_c, -1, 1)),
            jnp.where(first_col, col_ghost2, roll(fwd_c, 1, 1)),
        ]
        q2 = [axpy4([span[k], span_b[k], chord[k], chord_b[k]], near) for k in range(dof)]
        miss = (corner_kappa * col_ghost, corner_kappa * row_ghost)
        cross = miss[0] * jnp.where(last_row, near[0], near[1]) + miss[1] * jnp.where(last_col, near[2], near[3])
        row_z, col_z, row_q, col_q = (cross_ref[pl.ds((i * modes + m) * rows, rows), :] for i in range(4))
        products = (
            row_z * row_ghost + col_z * col_ghost,
            row_ghost * (2.0 * (row_q + miss[0]) + row_kappa * row_ghost)
            + col_ghost * (2.0 * col_q + col_kappa * col_ghost),
            dot(g, q2) + cross,
        )
        for which, product in enumerate(products):
            sum_ref[pl.ds((which * modes + m) * rows, rows), :] = product
        for k in range(dof):
            g_ref[at[k], :] = g[k]
            q2_ref[at[k], :] = q2[k]
        mine = (lane >> 1) == m
        return tuple(jnp.where(mine, roll(new, 2 * m + 1, 1), old) for new, old in zip(miss, carry))

    corners = (zero, zero)
    for m in range(modes):
        corners = body(m, corners)
    sums = jnp.concatenate([sum_of_rows(sum_ref, block * 8 * rows, rows) for block in range(3 * modes // 8)], axis=0)
    sums = jnp.concatenate(
        [first_ref[0:modes, :], first_ref[modes:3 * modes, :] + sums[0:2 * modes], sums[2 * modes:]], axis=0
    )
    sums = jnp.sum(jnp.transpose(sums), axis=0, keepdims=True)
    chunk = jnp.where(row % LINES == 0, sums[0:1], zero)
    for which, corner in enumerate(corners):
        far = roll(jnp.broadcast_to(corner[rows - 1:rows], (rows, cols)), cols // 2, 1)
        line = jnp.where(lane < cols // 2, corner[0:1], far)
        chunk = jnp.where(row % LINES == which + 1, line, chunk)

    def send(d, carry):
        chunk_ref[pl.ds(pl.multiple_of(d * rows, rows), rows), :] = chunk
        return carry

    lax.fori_loop(0, devices * LINES // rows, send, 0, unroll=8)


def last_kernel(dims, sizes, steps, part_ref, coef_ref, up_ref, down_ref, rim_ref,
                load_ref, z_ref, q_ref, g_ref, q2_ref,
                adjoint_hbm, residual_hbm, a_ref, b_ref, load_share_ref, q_share_ref, shares_ref, adjoint_ref, residual_ref, sems):
    modes, dof, rows, cols = dims
    slabs, subs = sizes
    devices = slabs * subs
    row, lane = tile_iota((rows, cols))
    per = dof * rows
    half = cols // 2

    shares_ref[0:devices * LINES, :] = part_ref[...]

    def lines(which):
        return shares_ref[pl.ds(which, devices, stride=LINES), :]

    miss_row, miss_col = lines(1), lines(2)
    wide = lax.broadcasted_iota(jnp.int32, (devices, cols), 1)
    swapped = roll(miss_row, half, 1)
    met_row = jnp.where(wide >= half, roll(swapped, -subs, 0), roll(swapped, subs, 0))
    met_col = jnp.where((wide & 1) == 0, roll(roll(miss_col, -1, 1), -1, 0), roll(roll(miss_col, 1, 1), 1, 0))
    total = jnp.sum(lines(0), axis=0, keepdims=True)
    missed = jnp.sum(miss_row * met_row + miss_col * met_col, axis=0, keepdims=True)
    big_row, big_lane = tile_iota((4 * modes, cols))
    spread = jnp.where(big_row == big_lane, total, 0.0)
    spread = spread + jnp.where(((big_lane & (half - 1)) >> 1) == big_row - 3 * modes, missed, 0.0)
    spread = times_ones(spread, False)
    m0, m1, m2, m3 = (spread[i * modes:(i + 1) * modes] for i in range(4))
    m1, m2, m3 = m1 / m0, m2 / m0, m3 / m0
    step0 = 1.0 / (1.0 - m1)
    square = step0 * step0
    beta = (m2 - m1 * m1) * square
    c0 = (m2 - m1) * square
    excess = beta * beta - (c0 * c0 * m1 + 2.0 * c0 * step0 * m2 + square * m3)
    inverse = 1.0 / (beta + excess)
    step1 = beta * inverse
    a_ref[...] = step0 + step1 * c0
    b_ref[...] = step1 * step0
    load_share_ref[...] = -m1 * step0 - step1 * c0
    q_share_ref[...] = step0 * (excess * inverse) + step1 * c0

    here = lax.axis_index("slab") * subs + lax.axis_index("sub")

    def line_of(device, which):
        device = lax.rem(device + devices, devices)
        return jnp.broadcast_to(part_ref[pl.ds(device * LINES + which, 1), :], (rows, cols))

    row_fixes = jnp.where(row == rows - 1, line_of(here + subs, 1), roll(line_of(here - subs, 1), half, 1))
    col_fixes = jnp.where((lane & 1) == 0, roll(line_of(here + 1, 2), -1, 1), roll(line_of(here - 1, 2), 1, 1))
    col_fixes = jnp.where(row == rows - 1, roll(col_fixes, half, 1), col_fixes)
    corner = ((row == 0) | (row == rows - 1)) & ((lane == 0) | (lane == cols - 1))
    count = modes // steps
    copies = []
    for m in range(modes):
        a = a_ref[m:m + 1, :]
        b = b_ref[m:m + 1, :]
        load_share = load_share_ref[m:m + 1, :]
        q_share = q_share_ref[m:m + 1, :]
        row_ghost = jnp.where(row == rows - 1, down_ref[m:m + 1, :], up_ref[m:m + 1, :])
        col_ghost = roll(rim_ref[...], -2 * m, 1)
        row_fix = b * jnp.where(corner, roll(row_fixes, -1 - 2 * m, 1), 0.0) + q_share * row_ghost
        col_fix = b * jnp.where(corner, roll(col_fixes, -1 - 2 * m, 1), 0.0) + q_share * col_ghost
        for k in range(dof):
            at = pl.ds(m * per + k * rows, rows)
            adjoint_ref[at, :] = a * z_ref[at, :] + b * g_ref[at, :]
            residual_ref[at, :] = (
                (load_share * load_ref[at, :] + q_share * q_ref[at, :])
                + (b * q2_ref[at, :] + (coef_ref[4 * dof + k] * row_fix + coef_ref[5 * dof + k] * col_fix))
            )
        if (m + 1) % count == 0:
            at = pl.ds((m + 1 - count) * per, count * per)
            for src, dst in ((adjoint_ref, adjoint_hbm), (residual_ref, residual_hbm)):
                copy = pltpu.make_async_copy(src.at[at, :], dst.at[at, :], sems.at[len(copies)])
                copy.start()
                copies.append(copy)
    for copy in copies:
        copy.wait()


def body_of(sizes):
    slabs, subs = sizes
    devices = slabs * subs
    axes = ("slab", "sub")
    paths = [matching(slabs, subs, along, parity) for along in (True, False) for parity in (0, 1)]

    def exchange(arrays):
        return [lax.ppermute(array, axes, path) for array, path in zip(arrays, paths)]

    vmem = pl.BlockSpec(memory_space=pltpu.VMEM)
    hbm = pl.BlockSpec(memory_space=pltpu.HBM)

    def body(mode_shapes, span_stiff, chord_stiff, span_geo, chord_geo, ground, chord_len):
        modes, dof, rows, cols = mode_shapes.shape
        dims = mode_shapes.shape
        count = modes * dof * rows

        def call(kernel, name, inputs, in_specs, outs, scratch, out_spec=vmem):
            return pl.pallas_call(
                kernel,
                out_shape=[jax.ShapeDtypeStruct(shape, F32) for shape in outs],
                in_specs=in_specs,
                out_specs=[out_spec] * len(outs),
                scratch_shapes=[pltpu.VMEM(s, F32) if isinstance(s, tuple) else s for s in scratch],
                compiler_params=pltpu.CompilerParams(vmem_limit_bytes=VMEM_LIMIT),
                name=name,
            )(*inputs)

        plane, planes, full = (rows, cols), (dof, rows, cols), (count, cols)
        row_shape, col_shape = (modes * dof + rows, cols), ((dof + 1) * rows, cols)
        parts = 2
        inputs = (mode_shapes.reshape(count, cols), span_stiff, chord_stiff, span_geo, chord_geo, chord_len)
        field, *coefs, row_even, row_odd, col_even, col_odd = call(
            lambda *refs: pack_kernel(dims, sizes, parts, *refs), "pack_rim",
            [pltpu.with_memory_space_constraint(x, pltpu.HBM) for x in inputs], [hbm] * 6,
            [(count + 8 * dof * rows, cols), (4, rows, cols), planes, planes, plane, plane, row_shape, row_shape, col_shape, col_shape],
            [pltpu.VMEM(full, mode_shapes.dtype), pltpu.SMEM(chord_len.shape, jnp.int32), pltpu.SemaphoreType.DMA((parts + 5,))],
        )
        rims = [row_even, row_odd, col_even, col_odd]
        met = exchange(rims)
        (inner,) = call(
            lambda *refs: inner_kernel(dims, *refs), "inner_load", (field, *coefs), [vmem] * 6, [full], [],
        )
        row_shape, col_shape = (2 * modes + rows, cols), (3 * rows, cols)
        load, z, qp, coef, *rims2 = call(
            lambda *refs: first_kernel(dims, *refs), "load_and_first",
            (inner, *coefs, ground, *rims, *met), [vmem] * 15,
            [full] * 3 + [(factor_place(dof, dof, 0), rows, cols), row_shape, row_shape, col_shape, col_shape],
            [(modes, cols), (modes, cols), ((modes + 1) * rows, cols), ((modes + 1) * rows, cols)],
        )
        met2 = exchange(rims2)
        gp, first, cross = call(
            lambda *refs: solve_kernel(dims, *refs), "solve_inner", (load, z, qp, coef), [vmem] * 4,
            [full, (3 * modes, cols), (4 * modes * rows, cols)], [((3 * modes + 1) * rows, cols)],
        )
        g, q2, chunk, up, down, rim = call(
            lambda *refs: second_kernel(dims, devices, *refs), "second_and_sums",
            (first, cross, gp, coef, *rims2, *met2), [vmem] * 12,
            [full] * 2 + [(devices * LINES, cols), (modes, cols), (modes, cols), plane],
            [(modes, cols)] * 2 + [((3 * modes + 1) * rows, cols)],
        )
        shares = lax.all_to_all(chunk.reshape(devices, LINES, cols), axes, 0, 0).reshape(devices * LINES, cols)
        steps = 4
        adjoint, residual = call(
            lambda *refs: last_kernel(dims, sizes, steps, *refs), "combine",
            (shares, coef, up, down, rim, load, z, qp, g, q2), [vmem] * 10, [full] * 2,
            [(modes, cols)] * 4 + [(devices * LINES + 8, cols), full, full, pltpu.SemaphoreType.DMA((2 * steps,))], hbm,
        )
        return adjoint.reshape(dims), residual.reshape(dims)

    return body


def solution(mesh):
    return jax.shard_map(
        body_of((mesh.shape["slab"], mesh.shape["sub"])),
        mesh=mesh,
        in_specs=(
            P(None, None, "slab", "sub"),
            P(None, "slab", "sub"),
            P(None, "slab", "sub"),
            P("slab", "sub"),
            P("slab", "sub"),
            P(None, "slab", "sub"),
            P(),
        ),
        out_specs=(P(None, None, "slab", "sub"), P(None, None, "slab", "sub")),
        check_vma=False,
    )
```

```python
import jax
import jax.numpy as jnp
from jax import lax
from jax.experimental import pallas as pl
from jax.experimental.pallas import tpu as pltpu
from jax.sharding import PartitionSpec as P

F32 = jnp.float32
VMEM_LIMIT = 24 * 1024 * 1024
LINES = 4


def matching(slabs, subs, along_slab, parity):
    pairs = []
    for s in range(slabs):
        for c in range(subs):
            here, count = (s, slabs) if along_slab else (c, subs)
            there = here + 1 if here % 2 == parity else here - 1
            if 0 <= there < count:
                target = (there, c) if along_slab else (s, there)
            elif along_slab:
                target = (s, c ^ 1) if subs % 2 == 0 else None
            else:
                target = (s, subs - 1 - c) if subs % 2 == 0 else None
            if target is not None:
                pairs.append((s * subs + c, target[0] * subs + target[1]))
    return pairs


def roll(value, shift, axis):
    size = value.shape[axis]
    if isinstance(shift, int):
        return pltpu.roll(value, shift % size, axis)
    return pltpu.roll(value, lax.rem(shift + size, size), axis)


def dot(left, right):
    total = left[0] * right[0]
    for k in range(1, len(left)):
        total = total + left[k] * right[k]
    return total


def axpy4(coefs, values):
    total = coefs[0] * values[0]
    for k in range(1, len(coefs)):
        total = total + coefs[k] * values[k]
    return total


def tile_iota(shape):
    return lax.broadcasted_iota(jnp.int32, shape, 0), lax.broadcasted_iota(jnp.int32, shape, 1)


def parities():
    return lax.rem(lax.axis_index("slab"), 2) == 0, lax.rem(lax.axis_index("sub"), 2) == 0


def pack_kernel(dims, sizes, parts, modes_hbm, span_hbm, chord_hbm, span_geo_hbm, chord_geo_hbm, len_hbm,
                field, live_ref, span_ref, chord_ref, span_geo_ref, chord_geo_ref, row_even, row_odd, col_even, col_odd,
                raw, len_ref, sems):
    modes, dof, rows, cols = dims
    row, lane = tile_iota((rows, cols))
    slab_even, sub_even = parities()
    per = dof * rows
    share = modes // parts
    fetches = [
        pltpu.make_async_copy(modes_hbm.at[pl.ds(i * share * per, share * per), :],
                              raw.at[pl.ds(i * share * per, share * per), :], sems.at[i])
        for i in range(parts)
    ]
    small = ((span_hbm, span_ref), (chord_hbm, chord_ref), (span_geo_hbm, span_geo_ref), (chord_geo_hbm, chord_geo_ref),
             (len_hbm, len_ref))
    others = [pltpu.make_async_copy(src, dst, sems.at[parts + i]) for i, (src, dst) in enumerate(small)]
    for copy in others + fetches:
        copy.start()
    for copy in others:
        copy.wait()

    stations = sizes[0] * rows
    row_start = lax.axis_index("slab") * rows
    col_start = lax.axis_index("sub") * cols

    def length(index):
        value = len_ref[jnp.clip(index, 0, stations - 1)]
        return jnp.where((index >= 0) & (index < stations), value, 0)

    lengths = [length(row_start + r) for r in range(-1, rows + 1)]
    own = jnp.zeros((rows, cols), jnp.int32)
    ahead = jnp.zeros((rows, cols), jnp.int32)
    for r in range(rows):
        own = jnp.where(row == r, lengths[r + 1], own)
        ahead = jnp.where(row == r, lengths[r + 2], ahead)
    column = col_start + lane
    up_live = (column < lengths[0]) & (column < lengths[1])
    left_live = (col_start < own) & (col_start > 0)
    live = ((column < own) & (column < ahead), column + 1 < own, up_live, left_live)
    for i, flags in enumerate(live):
        live_ref[i] = flags.astype(F32)

    packed = [jnp.zeros((rows, cols), F32) for k in range(dof)]
    for m in range(modes):
        if m % share == 0:
            fetches[m // share].wait()
        block = raw[m * per:(m + 1) * per, :].astype(F32)
        field[m * per:(m + 1) * per, :] = block
        mine = (lane >> 1) == m
        for k in range(dof):
            packed[k] = jnp.where(mine, roll(block[k * rows:(k + 1) * rows], 2 * m + 1, 1), packed[k])
        if m % 8 == 7:
            for k in range(dof):
                base = (m - 7) * per + k * rows
                first = field[pl.ds(base, 8, stride=per), :]
                last = field[pl.ds(base + rows - 1, 8, stride=per), :]
                out = k * modes + m - 7
                row_even[out:out + 8, :] = jnp.where(slab_even, last, first)
                row_odd[out:out + 8, :] = jnp.where(slab_even, first, last)
    field[modes * per:modes * per + rows, :] = jnp.zeros((rows, cols), F32)
    coef = jnp.zeros((rows, cols), F32)
    edge = jnp.zeros((rows, cols), F32)
    for k in range(dof + 1):
        span_plane = span_ref[k] if k < dof else span_geo_ref[...]
        chord_plane = chord_ref[k] if k < dof else chord_geo_ref[...]
        coef = jnp.where(row == k, span_plane[rows - 1:rows], coef)
        edge = jnp.where(lane == 2 * k, roll(chord_plane, 2 * k + 1, 1), edge)
    for k in range(dof):
        behind = roll(packed[k], -1, 1)
        col_even[k * rows:(k + 1) * rows, :] = jnp.where(sub_even, packed[k], behind)
        col_odd[k * rows:(k + 1) * rows, :] = jnp.where(sub_even, behind, packed[k])
    row_even[dof * modes:dof * modes + rows, :] = coef
    row_odd[dof * modes:dof * modes + rows, :] = coef
    col_even[dof * rows:(dof + 1) * rows, :] = edge
    col_odd[dof * rows:(dof + 1) * rows, :] = edge


def factor_blocks(blocks):
    count = len(blocks)
    scaled = [[None] * count for i in range(count)]
    factor = [[None] * count for i in range(count)]
    for j in range(count):
        running = blocks[j][j]
        for k in range(j):
            running = running - scaled[j][k] * factor[j][k]
        factor[j][j] = 1.0 / running
        for i in range(j + 1, count):
            running = blocks[i][j]
            for k in range(j):
                running = running - scaled[i][k] * factor[j][k]
            scaled[i][j] = running
            factor[i][j] = running * factor[j][j]
    return factor


def times_ones(value, transposed):
    high = value.astype(jnp.bfloat16)
    rest = value - high.astype(F32)
    middle = rest.astype(jnp.bfloat16)
    low = (rest - middle.astype(F32)).astype(jnp.bfloat16)
    pieces = jnp.concatenate([high, middle, low], axis=1)
    if transposed:
        ones = jnp.ones((8, pieces.shape[1]), jnp.bfloat16)
        return lax.dot_general(ones, pieces, (((1,), (1,)), ((), ())), preferred_element_type=F32)
    ones = jnp.ones((pieces.shape[1], value.shape[1]), jnp.bfloat16)
    return lax.dot_general(pieces, ones, (((1,), (0,)), ((), ())), preferred_element_type=F32)


def factor_place(dof, i, j):
    return 8 * dof + 3 + i * (i + 1) // 2 + j


def solve_blocks(factor, vector):
    count = len(vector)
    forward = []
    for i in range(count):
        running = vector[i]
        for j in range(i):
            running = running - factor(i, j) * forward[j]
        forward.append(running)
    backward = [None] * count
    for i in reversed(range(count)):
        running = forward[i] * factor(i, i)
        for j in range(i + 1, count):
            running = running - factor(j, i) * backward[j]
        backward[i] = running
    return backward


def inner_kernel(dims, modes_ref, live_ref, span_ref, chord_ref, span_geo_ref, chord_geo_ref, load_ref):
    modes, dof, rows, cols = dims
    row, lane = tile_iota((rows, cols))
    per = dof * rows
    first_row, last_row = row == 0, row == rows - 1
    first_col, last_col = lane == 0, lane == cols - 1
    zero = jnp.zeros((rows, cols), F32)
    span_inner = (live_ref[0] > 0.0) & jnp.logical_not(last_row)
    chord_inner = (live_ref[1] > 0.0) & jnp.logical_not(last_col)
    span = [jnp.where(span_inner, span_ref[k], zero) for k in range(dof)]
    chord = [jnp.where(chord_inner, chord_ref[k], zero) for k in range(dof)]
    span_b = [jnp.where(first_row, zero, roll(span[k], 1, 0)) for k in range(dof)]
    chord_b = [jnp.where(first_col, zero, roll(chord[k], 1, 1)) for k in range(dof)]
    span_geo = jnp.where(span_inner, span_geo_ref[...], zero)
    chord_geo = jnp.where(chord_inner, chord_geo_ref[...], zero)
    for m in range(modes):
        start = m * per
        v = [modes_ref[pl.ds(start + k * rows, rows), :] for k in range(dof)]
        jumps = [modes_ref[pl.ds(start + k * rows + 1, rows), :] - v[k] for k in range(dof)]
        span_w = jnp.where(last_row, zero, dot(jumps, jumps) * span_geo)
        jumps = [roll(v[k], -1, 1) - v[k] for k in range(dof)]
        chord_w = jnp.where(last_col, zero, dot(jumps, jumps) * chord_geo)
        span_wb, chord_wb = roll(span_w, 1, 0), roll(chord_w, 1, 1)
        for k in range(dof):
            load_ref[pl.ds(start + k * rows, rows), :] = (
                (span_b[k] * span_wb - span[k] * span_w) + (chord_b[k] * chord_wb - chord[k] * chord_w)
            )


def first_kernel(dims, inner_ref, live_ref, span_ref, chord_ref, span_geo_ref, chord_geo_ref, ground_ref,
                 row_even_out, row_odd_out, col_even_out, col_odd_out,
                 row_even_in, row_odd_in, col_even_in, col_odd_in,
                 load_ref, z_ref, q_ref, coef_ref, row_even, row_odd, col_even, col_odd,
                 up_ref, down_ref, rim_ref, rim2_ref):
    modes, dof, rows, cols = dims
    row, lane = tile_iota((rows, cols))
    slab_even, sub_even = parities()
    per = dof * rows
    span_live, chord_live, up_live, left_live = (live_ref[i] > 0.0 for i in range(4))

    def row_weight(arrived, sent):
        total = None
        for k in range(dof):
            jump = arrived[k * modes:(k + 1) * modes, :] - sent[k * modes:(k + 1) * modes, :]
            total = jump * jump if total is None else total + jump * jump
        return total

    def col_weight(arrived, sent):
        total = None
        for k in range(dof):
            jump = arrived[k * rows:(k + 1) * rows, :] - sent[k * rows:(k + 1) * rows, :]
            total = jump * jump if total is None else total + jump * jump
        return total

    even_weight = row_weight(row_even_in, row_even_out)
    odd_weight = row_weight(row_odd_in, row_odd_out)
    up_weight = jnp.where(slab_even, odd_weight, even_weight)
    down_weight = jnp.where(slab_even, even_weight, odd_weight)
    tail = dof * modes
    up_coef = jnp.where(slab_even, row_odd_in[tail:tail + rows, :], row_even_in[tail:tail + rows, :])
    up_ref[...] = jnp.where(live_ref[2, 0:1, :] > 0.0, up_weight * up_coef[dof:dof + 1], 0.0)
    down_ref[...] = jnp.where(live_ref[0, rows - 1:rows, :] > 0.0, down_weight * span_geo_ref[rows - 1:rows, :], 0.0)
    even_col = col_weight(col_even_in, col_even_out)
    odd_col = col_weight(col_odd_in, col_odd_out)
    left_coef = jnp.where(sub_even, col_odd_in[per:per + rows, :], col_even_in[per:per + rows, :])
    left_weight = jnp.where(sub_even, odd_col, even_col) * left_coef[:, 2 * dof:2 * dof + 1]
    right_weight = jnp.where(sub_even, even_col, odd_col) * chord_geo_ref[:, cols - 1:cols]
    left_weight = jnp.where(left_live, left_weight, 0.0)
    right_weight = jnp.where(live_ref[1, :, cols - 1:cols] > 0.0, right_weight, 0.0)
    lane_even = (lane & 1) == 0
    rim_weight = jnp.where(lane_even, left_weight, roll(right_weight, -1, 1))

    first_row, last_row = row == 0, row == rows - 1
    first_col, last_col = lane == 0, lane == cols - 1

    zero = jnp.zeros((rows, cols), F32)
    span, span_b, chord, chord_b = [], [], [], []
    for k in range(dof):
        span.append(jnp.where(span_live, span_ref[k], zero))
        up = jnp.where(up_live, up_coef[k:k + 1], zero)
        span_b.append(jnp.where(first_row, up, roll(span[k], 1, 0)))
        chord.append(jnp.where(chord_live, chord_ref[k], zero))
        left = jnp.where(left_live, left_coef[:, 2 * k:2 * k + 1], zero)
        chord_b.append(jnp.where(first_col, left, roll(chord[k], 1, 1)))
    blocks = [[None] * dof for i in range(dof)]
    for i in range(dof):
        for j in range(i + 1):
            entry = span[i] * span[j] + span_b[i] * span_b[j] + chord[i] * chord[j] + chord_b[i] * chord_b[j]
            blocks[i][j] = entry + ground_ref[i] if i == j else entry
    factor = factor_blocks(blocks)
    for i in range(dof):
        for j in range(i + 1):
            coef_ref[factor_place(dof, i, j)] = factor[i][j]
    row_rim = [jnp.where(last_row, span[k], jnp.where(first_row, span_b[k], zero)) for k in range(dof)]
    col_rim = [jnp.where(last_col, chord[k], jnp.where(first_col, chord_b[k], zero)) for k in range(dof)]
    row_sign = [jnp.where(last_row, -row_rim[k], row_rim[k]) for k in range(dof)]
    col_sign = [jnp.where(last_col, -col_rim[k], col_rim[k]) for k in range(dof)]
    row_inv = solve_blocks(lambda i, j: factor[i][j], row_rim)
    col_inv = solve_blocks(lambda i, j: factor[i][j], col_rim)
    for group, planes in enumerate((span, span_b, chord, chord_b, row_rim, col_rim, row_inv, col_inv)):
        for k in range(dof):
            coef_ref[group * dof + k] = planes[k]
    row_kappa = dot(row_rim, row_inv)
    col_kappa = dot(col_rim, col_inv)
    coef_ref[8 * dof] = dot(row_rim, col_inv)
    coef_ref[8 * dof + 1] = row_kappa
    coef_ref[8 * dof + 2] = col_kappa

    def planes_of(group):
        return [coef_ref[group * dof + k] for k in range(dof)]

    def body(m, carry):
        start = m * per
        row_w = jnp.where(last_row, down_ref[pl.ds(m, 1), :], up_ref[pl.ds(m, 1), :])
        col_w = roll(rim_weight, -2 * m, 1)
        span, span_b, chord, chord_b = (planes_of(i) for i in range(4))
        load = [
            inner_ref[pl.ds(start + k * rows, rows), :] + (row_sign[k] * row_w + col_sign[k] * col_w)
            for k in range(dof)
        ]
        z = solve_blocks(lambda i, j: coef_ref[factor_place(dof, i, j)], load)
        fwd_s, bwd_s, fwd_c, bwd_c = dot(span, z), dot(span_b, z), dot(chord, z), dot(chord_b, z)
        near = [
            jnp.where(last_row, zero, roll(bwd_s, -1, 0)),
            jnp.where(first_row, zero, roll(fwd_s, 1, 0)),
            jnp.where(last_col, zero, roll(bwd_c, -1, 1)),
            jnp.where(first_col, zero, roll(fwd_c, 1, 1)),
        ]
        q = [axpy4([span[k], span_b[k], chord[k], chord_b[k]], near) for k in range(dof)]
        for k in range(dof):
            at = pl.ds(start + k * rows, rows)
            load_ref[at, :] = load[k]
            z_ref[at, :] = z[k]
            q_ref[at, :] = q[k]
        at = pl.ds(m * rows, rows)
        rim_ref[at, :] = jnp.where(last_row, fwd_s, bwd_s)
        rim2_ref[at, :] = dot(planes_of(6), q)
        mine = (lane >> 1) == m
        col_z = roll(jnp.where(last_col, fwd_c, bwd_c), 2 * m + 1, 1)
        col_g = roll(dot(planes_of(7), q), 2 * m + 1, 1)
        return jnp.where(mine, col_z, carry[0]), jnp.where(mine, col_g, carry[1])

    col_z, col_g = zero, zero
    for m in range(modes):
        col_z, col_g = body(m, (col_z, col_g))
    for which, packed in enumerate((col_z, col_g, roll(col_kappa, 1, 1))):
        behind = roll(packed, -1, 1)
        col_even[which * rows:(which + 1) * rows, :] = jnp.where(sub_even, packed, behind)
        col_odd[which * rows:(which + 1) * rows, :] = jnp.where(sub_even, behind, packed)
    for which, ref in enumerate((rim_ref, rim2_ref)):
        for block in range(modes // 8):
            first = ref[pl.ds(block * 8 * rows, 8, stride=rows), :]
            last = ref[pl.ds(block * 8 * rows + rows - 1, 8, stride=rows), :]
            out = which * modes + block * 8
            row_even[out:out + 8, :] = jnp.where(slab_even, last, first)
            row_odd[out:out + 8, :] = jnp.where(slab_even, first, last)
    first = jnp.where(first_row, row_kappa[0:1], zero)
    last = jnp.where(first_row, row_kappa[rows - 1:rows], zero)
    row_even[2 * modes:2 * modes + rows, :] = jnp.where(slab_even, last, first)
    row_odd[2 * modes:2 * modes + rows, :] = jnp.where(slab_even, first, last)


def solve_kernel(dims, load_ref, z_ref, q_ref, coef_ref, g_ref, first_ref, cross_ref, sum_ref):
    modes, dof, rows, cols = dims
    for m in range(modes):
        at = [pl.ds((m * dof + k) * rows, rows) for k in range(dof)]
        q = [q_ref[at[k], :] for k in range(dof)]
        g = solve_blocks(lambda i, j: coef_ref[factor_place(dof, i, j)], q)
        for k in range(dof):
            g_ref[at[k], :] = g[k]
        z, load = [z_ref[at[k], :] for k in range(dof)], [load_ref[at[k], :] for k in range(dof)]
        for which, (left, right) in enumerate(((z, load), (z, q), (g, q))):
            sum_ref[pl.ds((which * modes + m) * rows, rows), :] = dot(left, right)
        for which, (group, field) in enumerate(((4, z), (5, z), (6, q), (7, q))):
            planes = [coef_ref[group * dof + k] for k in range(dof)]
            cross_ref[pl.ds((which * modes + m) * rows, rows), :] = dot(planes, field)
    for block in range(3 * modes // 8):
        first_ref[block * 8:block * 8 + 8, :] = sum_of_rows(sum_ref, block * 8 * rows, rows)


def sum_of_rows(ref, base, rows):
    total = ref[pl.ds(base, 8, stride=rows), :]
    for r in range(1, rows):
        total = total + ref[pl.ds(base + r, 8, stride=rows), :]
    return total


def second_kernel(dims, devices, first_ref, cross_ref, gp_ref, coef_ref,
                  row_even_out, row_odd_out, col_even_out, col_odd_out,
                  row_even_in, row_odd_in, col_even_in, col_odd_in,
                  g_ref, q2_ref, chunk_ref, up_ref, down_ref, rim_ref,
                  up2_ref, down2_ref, sum_ref):
    modes, dof, rows, cols = dims
    row, lane = tile_iota((rows, cols))
    slab_even, sub_even = parities()
    per = dof * rows
    first_row, last_row = row == 0, row == rows - 1
    first_col, last_col = lane == 0, lane == cols - 1
    lane_even = (lane & 1) == 0
    zero = jnp.zeros((rows, cols), F32)

    def pick(flag, even, odd, start, size):
        return jnp.where(flag, even[start:start + size, :], odd[start:start + size, :])

    up_flag = jnp.logical_not(slab_even)
    left_flag = jnp.logical_not(sub_even)
    up_ref[...] = pick(up_flag, row_even_in, row_odd_in, 0, modes)
    down_ref[...] = pick(slab_even, row_even_in, row_odd_in, 0, modes)
    up2_ref[...] = (
        pick(up_flag, row_even_in, row_odd_in, modes, modes)
        + pick(up_flag, row_even_in, row_odd_in, 2 * modes, 1) * pick(up_flag, row_even_out, row_odd_out, 0, modes)
    )
    down2_ref[...] = (
        pick(slab_even, row_even_in, row_odd_in, modes, modes)
        + pick(slab_even, row_even_in, row_odd_in, 2 * modes, 1) * pick(slab_even, row_even_out, row_odd_out, 0, modes)
    )

    def merge(left, right):
        return jnp.where(lane_even, left, roll(right, -1, 1))

    def second_col(flag):
        kappa = pick(flag, col_even_in, col_odd_in, 2 * rows, rows)[:, 0:1]
        return pick(flag, col_even_in, col_odd_in, rows, rows) + kappa * pick(flag, col_even_out, col_odd_out, 0, rows)

    rim = merge(pick(left_flag, col_even_in, col_odd_in, 0, rows), pick(sub_even, col_even_in, col_odd_in, 0, rows))
    rim2 = merge(second_col(left_flag), second_col(sub_even))
    corner_kappa, row_kappa, col_kappa = (coef_ref[8 * dof + i] for i in range(3))
    rim_ref[...] = rim

    def planes_of(group):
        return [coef_ref[group * dof + k] for k in range(dof)]

    def body(m, carry):
        start = m * per
        at = [pl.ds(start + k * rows, rows) for k in range(dof)]
        row_ghost = jnp.where(last_row, down_ref[pl.ds(m, 1), :], up_ref[pl.ds(m, 1), :])
        col_ghost = roll(rim, -2 * m, 1)
        col_ghost2 = roll(rim2, -2 * m, 1)
        row_inv, col_inv = planes_of(6), planes_of(7)
        g = [gp_ref[at[k], :] + (row_inv[k] * row_ghost + col_inv[k] * col_ghost) for k in range(dof)]
        span, span_b, chord, chord_b = (planes_of(i) for i in range(4))
        fwd_s, bwd_s, fwd_c, bwd_c = dot(span, g), dot(span_b, g), dot(chord, g), dot(chord_b, g)
        near = [
            jnp.where(last_row, down2_ref[pl.ds(m, 1), :], roll(bwd_s, -1, 0)),
            jnp.where(first_row, up2_ref[pl.ds(m, 1), :], roll(fwd_s, 1, 0)),
            jnp.where(last_col, col_ghost2, roll(bwd_c, -1, 1)),
            jnp.where(first_col, col_ghost2, roll(fwd_c, 1, 1)),
        ]
        q2 = [axpy4([span[k], span_b[k], chord[k], chord_b[k]], near) for k in range(dof)]
        miss = (corner_kappa * col_ghost, corner_kappa * row_ghost)
        cross = miss[0] * jnp.where(last_row, near[0], near[1]) + miss[1] * jnp.where(last_col, near[2], near[3])
        row_z, col_z, row_q, col_q = (cross_ref[pl.ds((i * modes + m) * rows, rows), :] for i in range(4))
        products = (
            row_z * row_ghost + col_z * col_ghost,
            row_ghost * (2.0 * (row_q + miss[0]) + row_kappa * row_ghost)
            + col_ghost * (2.0 * col_q + col_kappa * col_ghost),
            dot(g, q2) + cross,
        )
        for which, product in enumerate(products):
            sum_ref[pl.ds((which * modes + m) * rows, rows), :] = product
        for k in range(dof):
            g_ref[at[k], :] = g[k]
            q2_ref[at[k], :] = q2[k]
        mine = (lane >> 1) == m
        return tuple(jnp.where(mine, roll(new, 2 * m + 1, 1), old) for new, old in zip(miss, carry))

    corners = (zero, zero)
    for m in range(modes):
        corners = body(m, corners)
    sums = jnp.concatenate([sum_of_rows(sum_ref, block * 8 * rows, rows) for block in range(3 * modes // 8)], axis=0)
    sums = jnp.concatenate(
        [first_ref[0:modes, :], first_ref[modes:3 * modes, :] + sums[0:2 * modes], sums[2 * modes:]], axis=0
    )
    sums = jnp.sum(jnp.transpose(sums), axis=0, keepdims=True)
    chunk = jnp.where(row % LINES == 0, sums[0:1], zero)
    for which, corner in enumerate(corners):
        far = roll(jnp.broadcast_to(corner[rows - 1:rows], (rows, cols)), cols // 2, 1)
        line = jnp.where(lane < cols // 2, corner[0:1], far)
        chunk = jnp.where(row % LINES == which + 1, line, chunk)

    def send(d, carry):
        chunk_ref[pl.ds(pl.multiple_of(d * rows, rows), rows), :] = chunk
        return carry

    lax.fori_loop(0, devices * LINES // rows, send, 0, unroll=8)


def last_kernel(dims, sizes, steps, part_ref, coef_ref, up_ref, down_ref, rim_ref,
                load_ref, z_ref, q_ref, g_ref, q2_ref,
                adjoint_hbm, residual_hbm, a_ref, b_ref, load_share_ref, q_share_ref, shares_ref, adjoint_ref, residual_ref, sems):
    modes, dof, rows, cols = dims
    slabs, subs = sizes
    devices = slabs * subs
    row, lane = tile_iota((rows, cols))
    per = dof * rows
    half = cols // 2

    shares_ref[0:devices * LINES, :] = part_ref[...]

    def lines(which):
        return shares_ref[pl.ds(which, devices, stride=LINES), :]

    miss_row, miss_col = lines(1), lines(2)
    wide = lax.broadcasted_iota(jnp.int32, (devices, cols), 1)
    swapped = roll(miss_row, half, 1)
    met_row = jnp.where(wide >= half, roll(swapped, -subs, 0), roll(swapped, subs, 0))
    met_col = jnp.where((wide & 1) == 0, roll(roll(miss_col, -1, 1), -1, 0), roll(roll(miss_col, 1, 1), 1, 0))
    total = jnp.sum(lines(0), axis=0, keepdims=True)
    missed = jnp.sum(miss_row * met_row + miss_col * met_col, axis=0, keepdims=True)
    big_row, big_lane = tile_iota((4 * modes, cols))
    spread = jnp.where(big_row == big_lane, total, 0.0)
    spread = spread + jnp.where(((big_lane & (half - 1)) >> 1) == big_row - 3 * modes, missed, 0.0)
    spread = times_ones(spread, False)
    m0, m1, m2, m3 = (spread[i * modes:(i + 1) * modes] for i in range(4))
    m1, m2, m3 = m1 / m0, m2 / m0, m3 / m0
    step0 = 1.0 / (1.0 - m1)
    square = step0 * step0
    beta = (m2 - m1 * m1) * square
    c0 = (m2 - m1) * square
    excess = beta * beta - (c0 * c0 * m1 + 2.0 * c0 * step0 * m2 + square * m3)
    inverse = 1.0 / (beta + excess)
    step1 = beta * inverse
    a_ref[...] = step0 + step1 * c0
    b_ref[...] = step1 * step0
    load_share_ref[...] = -m1 * step0 - step1 * c0
    q_share_ref[...] = step0 * (excess * inverse) + step1 * c0

    here = lax.axis_index("slab") * subs + lax.axis_index("sub")

    def line_of(device, which):
        device = lax.rem(device + devices, devices)
        return jnp.broadcast_to(part_ref[pl.ds(device * LINES + which, 1), :], (rows, cols))

    row_fixes = jnp.where(row == rows - 1, line_of(here + subs, 1), roll(line_of(here - subs, 1), half, 1))
    col_fixes = jnp.where((lane & 1) == 0, roll(line_of(here + 1, 2), -1, 1), roll(line_of(here - 1, 2), 1, 1))
    col_fixes = jnp.where(row == rows - 1, roll(col_fixes, half, 1), col_fixes)
    corner = ((row == 0) | (row == rows - 1)) & ((lane == 0) | (lane == cols - 1))
    count = modes // steps
    copies = []

    def store(m, src, dst):
        if (m + 1) % count == 0:
            at = pl.ds((m + 1 - count) * per, count * per)
            copy = pltpu.make_async_copy(src.at[at, :], dst.at[at, :], sems.at[len(copies)])
            copy.start()
            copies.append(copy)

    for m in range(modes):
        a = a_ref[m:m + 1, :]
        b = b_ref[m:m + 1, :]
        for k in range(dof):
            at = pl.ds(m * per + k * rows, rows)
            adjoint_ref[at, :] = a * z_ref[at, :] + b * g_ref[at, :]
        store(m, adjoint_ref, adjoint_hbm)
    for m in range(modes):
        b = b_ref[m:m + 1, :]
        load_share = load_share_ref[m:m + 1, :]
        q_share = q_share_ref[m:m + 1, :]
        row_ghost = jnp.where(row == rows - 1, down_ref[m:m + 1, :], up_ref[m:m + 1, :])
        col_ghost = roll(rim_ref[...], -2 * m, 1)
        row_fix = b * jnp.where(corner, roll(row_fixes, -1 - 2 * m, 1), 0.0) + q_share * row_ghost
        col_fix = b * jnp.where(corner, roll(col_fixes, -1 - 2 * m, 1), 0.0) + q_share * col_ghost
        for k in range(dof):
            at = pl.ds(m * per + k * rows, rows)
            residual_ref[at, :] = (
                (load_share * load_ref[at, :] + q_share * q_ref[at, :])
                + (b * q2_ref[at, :] + (coef_ref[4 * dof + k] * row_fix + coef_ref[5 * dof + k] * col_fix))
            )
        store(m, residual_ref, residual_hbm)
    for copy in copies:
        copy.wait()


def body_of(sizes):
    slabs, subs = sizes
    devices = slabs * subs
    axes = ("slab", "sub")
    paths = [matching(slabs, subs, along, parity) for along in (True, False) for parity in (0, 1)]

    def exchange(arrays):
        return [lax.ppermute(array, axes, path) for array, path in zip(arrays, paths)]

    vmem = pl.BlockSpec(memory_space=pltpu.VMEM)
    hbm = pl.BlockSpec(memory_space=pltpu.HBM)

    def body(mode_shapes, span_stiff, chord_stiff, span_geo, chord_geo, ground, chord_len):
        modes, dof, rows, cols = mode_shapes.shape
        dims = mode_shapes.shape
        count = modes * dof * rows

        def call(kernel, name, inputs, in_specs, outs, scratch, out_spec=vmem):
            return pl.pallas_call(
                kernel,
                out_shape=[jax.ShapeDtypeStruct(shape, F32) for shape in outs],
                in_specs=in_specs,
                out_specs=[out_spec] * len(outs),
                scratch_shapes=[pltpu.VMEM(s, F32) if isinstance(s, tuple) else s for s in scratch],
                compiler_params=pltpu.CompilerParams(vmem_limit_bytes=VMEM_LIMIT),
                name=name,
            )(*inputs)

        plane, planes, full = (rows, cols), (dof, rows, cols), (count, cols)
        row_shape, col_shape = (modes * dof + rows, cols), ((dof + 1) * rows, cols)
        parts = 2
        inputs = (mode_shapes.reshape(count, cols), span_stiff, chord_stiff, span_geo, chord_geo, chord_len)
        field, *coefs, row_even, row_odd, col_even, col_odd = call(
            lambda *refs: pack_kernel(dims, sizes, parts, *refs), "pack_rim",
            [pltpu.with_memory_space_constraint(x, pltpu.HBM) for x in inputs], [hbm] * 6,
            [(count + 8 * dof * rows, cols), (4, rows, cols), planes, planes, plane, plane, row_shape, row_shape, col_shape, col_shape],
            [pltpu.VMEM(full, mode_shapes.dtype), pltpu.SMEM(chord_len.shape, jnp.int32), pltpu.SemaphoreType.DMA((parts + 5,))],
        )
        rims = [row_even, row_odd, col_even, col_odd]
        met = exchange(rims)
        (inner,) = call(
            lambda *refs: inner_kernel(dims, *refs), "inner_load", (field, *coefs), [vmem] * 6, [full], [],
        )
        row_shape, col_shape = (2 * modes + rows, cols), (3 * rows, cols)
        load, z, qp, coef, *rims2 = call(
            lambda *refs: first_kernel(dims, *refs), "load_and_first",
            (inner, *coefs, ground, *rims, *met), [vmem] * 15,
            [full] * 3 + [(factor_place(dof, dof, 0), rows, cols), row_shape, row_shape, col_shape, col_shape],
            [(modes, cols), (modes, cols), ((modes + 1) * rows, cols), ((modes + 1) * rows, cols)],
        )
        met2 = exchange(rims2)
        gp, first, cross = call(
            lambda *refs: solve_kernel(dims, *refs), "solve_inner", (load, z, qp, coef), [vmem] * 4,
            [full, (3 * modes, cols), (4 * modes * rows, cols)], [((3 * modes + 1) * rows, cols)],
        )
        g, q2, chunk, up, down, rim = call(
            lambda *refs: second_kernel(dims, devices, *refs), "second_and_sums",
            (first, cross, gp, coef, *rims2, *met2), [vmem] * 12,
            [full] * 2 + [(devices * LINES, cols), (modes, cols), (modes, cols), plane],
            [(modes, cols)] * 2 + [((3 * modes + 1) * rows, cols)],
        )
        shares = lax.all_to_all(chunk.reshape(devices, LINES, cols), axes, 0, 0).reshape(devices * LINES, cols)
        steps = 4
        adjoint, residual = call(
            lambda *refs: last_kernel(dims, sizes, steps, *refs), "combine",
            (shares, coef, up, down, rim, load, z, qp, g, q2), [vmem] * 10, [full] * 2,
            [(modes, cols)] * 4 + [(devices * LINES + 8, cols), full, full, pltpu.SemaphoreType.DMA((2 * steps,))], hbm,
        )
        return adjoint.reshape(dims), residual.reshape(dims)

    return body


def solution(mesh):
    return jax.shard_map(
        body_of((mesh.shape["slab"], mesh.shape["sub"])),
        mesh=mesh,
        in_specs=(
            P(None, None, "slab", "sub"),
            P(None, "slab", "sub"),
            P(None, "slab", "sub"),
            P("slab", "sub"),
            P("slab", "sub"),
            P(None, "slab", "sub"),
            P(),
        ),
        out_specs=(P(None, None, "slab", "sub"), P(None, None, "slab", "sub")),
        check_vma=False,
    )
```
